512 devices in a mesh: rep: 16 (over x, y_lo), ep: 32 (over z, y_hi, core).
Axes of the slice: x: 4, y: 8 (y_hi: 2, y_lo: 4; y = y_hi * 4 + y_lo), z: 8, core: 2. Of those that a mesh axis runs over, the one named last changes fastest.
Arguments:
- cotangent: bfloat16 [65536, 1536], P(('rep', 'ep')), may hold values from -12 to 12
- expert_ids: int32 [65536, 4], P(('rep', 'ep')), may hold values from 0 to 31, all different within a row; in each aligned block of 128 rows (0 to 127, 128 to 255, ...) at most 32 rows name the same one
- route_weight: bfloat16 [65536, 4], P(('rep', 'ep')), may hold values from 0.049804688 to 0.59765625
- hidden: bfloat16 [16, 32, 32, 32, 1024], P('rep', 'ep'), may hold values from -0.119628906 to 0.119628906
- down_weight: bfloat16 [32, 1024, 1536], P('ep', 'rep'), may hold values from -0.1875 to 0.1875
Outputs:
- router_grad: float32 [65536, 4], P(('rep', 'ep'))
- hidden_grad: bfloat16 [16, 32, 32, 32, 1024], P('rep', 'ep')
- down_grad: bfloat16 [32, 1024, 1536], P('ep', 'rep')
The draws below stay inside these ranges and needn't reach their ends.
Inputs may be any that keep to these rules, and one draw needn't show every extreme that they name: `expert_ids`: A token names 4 different experts; within the 128 tokens of one device no expert is named more than 32 times, and 32 is reached in some device.
All inputs are finite; a program needn't handle non-finite values.
Results may differ from the reference program's by a relative error of at most 0.022.
Values may be sent and summed in bfloat16 or wider, within the bound.
A program may use at most 64 MiB of HBM per device.

```python
import math
import jax
import jax.numpy as jnp
import numpy as np
from jax import lax

D = 1536
F = 1024
TOP = 4
TOK_DEV = 128
EXPERTS = 32
CAP = 32
TOKENS = 65536
N_REP = 16
N_EP = 32


def block_levels(stream_key, shape, pieces, least, top_value):
    level, own = 1.0, jax.random.fold_in(stream_key, 6)
    for dim, parts in pieces:
        steps = jnp.exp(jax.random.uniform(jax.random.fold_in(own, dim), (parts,), jnp.float32, least / len(pieces), top_value / len(pieces)))
        level = level * jnp.repeat(steps, shape[dim] // parts).reshape([-1 if axis == dim else 1 for axis in range(len(shape))])
    return level


def assign_block(rng, own, number, rows, count, top, bound, skew):
    order = jax.random.permutation(rng, count)
    crowded, ordinary = load_shares(count, rows * top, bound, skew, True), load_shares(count, rows * top, bound, skew, False)
    places = jnp.arange(count)

    def named(lengths, turn):
        used = int((lengths > 0).sum())
        fixed = max(1, used // 4)
        passed = fixed + (places - fixed + turn * (used - fixed)) % max(1, count - fixed)
        return jnp.zeros((count,), jnp.int32).at[order[jnp.where(places < fixed, places, passed)]].set(jnp.asarray(lengths, jnp.int32))

    lengths = jnp.where(number % 4 == 0, named(crowded, number // 4), named(ordinary, number - number // 4 - 1))
    mixed = jax.random.permutation(jax.random.fold_in(own, 3), count)
    giver, taker = mixed[0:count // 2 * 2:2], mixed[1:count // 2 * 2:2]
    room = jnp.minimum(lengths[giver] - 1, bound - lengths[taker]) // 2
    room = jnp.where((giver == order[0]) | (taker == order[0]) | (lengths[taker] == 0), 0, jnp.maximum(room, 0))
    passed = jax.random.randint(jax.random.fold_in(own, 4), (count // 2,), 0, 1 << 20) % (room + 1)
    lengths = lengths.at[giver].add(-passed).at[taker].add(passed)
    items = jnp.searchsorted(jnp.cumsum(lengths), jnp.arange(rows * top), side="right").astype(jnp.int32)
    grid = items.reshape(top, rows).T
    grid = grid[jax.random.permutation(jax.random.fold_in(own, 1), rows)]
    turn = jax.random.randint(jax.random.fold_in(own, 2), (rows, 1), 0, top)
    return jnp.take_along_axis(grid, (jnp.arange(top)[None, :] + turn) % top, axis=1)


def load_shares(number_of, total, bound, lean, full):
    loads = [(1 << 20) // math.isqrt(rank ** lean) + 1 for rank in range(1, number_of + 1)]
    largest = bound if full else min(bound, max(-(-total // number_of), total * loads[0] // sum(loads)))
    least = 1 if total - largest >= number_of - 1 else 0
    counts, spare = [largest] + [least] * (number_of - 1), total - largest - least * (number_of - 1)
    while spare > 0:
        movable = [i for i in range(1, number_of) if counts[i] < largest] or [i for i in range(1, number_of) if counts[i] < bound]
        whole, budget = sum([loads[i] for i in movable]), spare
        for i in movable:
            more = min(bound - counts[i], max(1, budget * loads[i] // whole), spare)
            counts[i] = counts[i] + more
            spare = spare - more
    return np.array(counts)


def scatter_about(rng, dims, deviation, bound, cuts=(), held_as=jnp.bfloat16):
    gain = block_levels(rng, dims, cuts, -0.22, 0.18) if cuts else 1.0
    entries = jax.random.normal(rng, dims, jnp.float32) * deviation * gain
    return jnp.minimum(jnp.maximum(entries, -bound), bound).astype(held_as)


def setup_inputs(seed: int = 0) -> dict:
    splits = jax.random.split(jax.random.key(seed), 6)
    cotangent = scatter_about(splits[0], (TOKENS, D), 2.0, 12.0, ((0, 512),))
    expert_ids_keys = jax.random.split(jax.random.fold_in(splits[1], 1), TOKENS // TOK_DEV)
    expert_ids_turns = jax.random.permutation(jax.random.fold_in(splits[1], 3), TOKENS // TOK_DEV)
    expert_ids = jax.vmap(lambda own, number: assign_block(jax.random.fold_in(splits[1], 2), own, number, TOK_DEV, EXPERTS, TOP, CAP, 2))(expert_ids_keys, expert_ids_turns).reshape((TOKENS, TOP))
    route_weight = jnp.clip(0.049804688 + 0.54785156 * jax.random.uniform(splits[2], (TOKENS, TOP), jnp.float32) ** block_levels(splits[2], (TOKENS, TOP), ((0, 512),), -0.2, 0.2), 0.049804688, 0.59765625).astype(jnp.bfloat16)
    hidden = scatter_about(splits[3], (N_REP, EXPERTS, N_EP, CAP, F), 0.02, 0.119628906, ((0, 16), (1, 32)))
    down_weight = scatter_about(splits[4], (EXPERTS, F, D), F ** -0.5, 0.1875, ((0, 32), (1, 16)))
    return {"cotangent": cotangent, "expert_ids": expert_ids, "route_weight": route_weight, "hidden": hidden, "down_weight": down_weight}


def reference(cotangent, expert_ids, route_weight, hidden, down_weight):
    slot_count = TOK_DEV * TOP
    flat_ids = expert_ids.reshape(N_REP, N_EP, slot_count)
    labels = jnp.arange(EXPERTS, dtype=jnp.int32)
    one_hot = (flat_ids[..., None] == labels).astype(jnp.int32)
    slot_rank = jnp.sum((jnp.cumsum(one_hot, axis=2) - one_hot) * one_hot, axis=3)
    destination = (flat_ids * CAP + slot_rank).astype(jnp.int32)
    token_index = jnp.arange(slot_count, dtype=jnp.int32) // TOP
    rows_all = cotangent.reshape(N_REP, N_EP, TOK_DEV, D)
    weights_all = route_weight.reshape(N_REP, N_EP, slot_count)
    source_index = jnp.broadcast_to(jnp.arange(N_EP, dtype=jnp.int32)[:, None], (N_EP, slot_count))
    weight_full = down_weight.astype(jnp.float32)

    def one_group(total, inputs):
        group_rows, group_weights, group_dest, group_hidden = inputs
        routed = jnp.zeros((N_EP, EXPERTS * CAP, D), cotangent.dtype)
        routed = routed.at[source_index, group_dest].set(group_rows[:, token_index])
        routed_weight = jnp.zeros((N_EP, EXPERTS * CAP), route_weight.dtype)
        routed_weight = routed_weight.at[source_index, group_dest].set(group_weights)
        routed = routed.reshape(N_EP, EXPERTS, CAP, D).transpose(1, 0, 2, 3).astype(jnp.float32)
        routed_weight = routed_weight.reshape(N_EP, EXPERTS, CAP).transpose(1, 0, 2).astype(jnp.float32)
        backward = jnp.einsum("escd,efd->escf", routed, weight_full)
        saved = group_hidden.astype(jnp.float32)
        hidden_grad = (routed_weight[..., None] * backward).astype(jnp.bfloat16)
        score = jnp.sum(saved * backward, axis=3)
        weighted = (routed_weight[..., None] * routed).astype(jnp.bfloat16)
        weighted = lax.optimization_barrier(weighted).astype(jnp.float32)
        partial_grad = jnp.einsum("escf,escd->efd", saved, weighted).astype(jnp.bfloat16)
        partial_grad = lax.optimization_barrier(partial_grad).astype(jnp.float32)
        flat_score = score.transpose(1, 0, 2).reshape(N_EP, EXPERTS * CAP)
        router_part = flat_score[source_index, group_dest]
        return total + partial_grad, (hidden_grad, router_part)

    start_total = jnp.zeros((EXPERTS, F, D), jnp.float32)
    total, outputs = lax.scan(one_group, start_total, (rows_all, weights_all, destination, hidden))
    hidden_grad, router_part = outputs
    router_grad = router_part.reshape(TOKENS, TOP)
    return router_grad, hidden_grad, total.astype(jnp.bfloat16)
```

```python
import functools

import jax
import jax.numpy as jnp
from jax import lax
from jax.experimental import pallas as pl
from jax.experimental.pallas import tpu as pltpu
from jax.sharding import PartitionSpec as P

MESH = pl.DeviceIdType.MESH
BF, F32 = jnp.bfloat16, jnp.float32
NT = (((1,), (1,)), ((), ()))
CHUNKS = 4


def remote(src, dst, send, recv, device):
    return pltpu.make_async_remote_copy(
        src_ref=src, dst_ref=dst, send_sem=send, recv_sem=recv, device_id=device, device_id_type=MESH
    )


def kernel(
    ct, ids, rw, hid_in, dw, rg, hg_out, dg_out,
    G, MT, PP, WR, WS, S, R, WB, hid, hidT, WG, back, PB, TA, TB, OWN, XH, XF, YB, YO, YR, DG, HG,
    SCB, L1, TT, L2, CODE,
    ld, out_sem, ms, mr, ys, yr, zs, zr, cs, cr, wys, wyr, wxs, wxr, xhs, xhr, xfs, xfr, yls, ylr,
    s1s, s1r, s2s, s2r,
):
    nc = G.shape[2]
    W = G.shape[4]
    rep, ep = lax.axis_index("rep"), lax.axis_index("ep")
    x, yl = rep // 4, rep % 4
    z, h, core = ep // 4, (ep // 2) % 2, ep % 2
    other = 1 - core
    ph = 1 - h

    def z_dev(k):
        return (rep, ((z + k + 8) % 8) * 4 + h * 2 + core)

    def x_dev(k):
        return (((x + k + 4) % 4) * 4 + yl, ep)

    def yl_dev(k):
        return (x * 4 + (yl + k) % 4, ep)

    def hc_dev(m):
        hh = ph if m // 2 else h
        cc = other if m % 2 else core
        return (rep, z * 4 + hh * 2 + cc)

    core_dev, y_dev = hc_dev(1), hc_dev(2)

    loads = []
    for c in range(nc):
        loads.append(pltpu.make_async_copy(ct.at[:, pl.ds(c * W, W)], G.at[z, h, c], ld.at[c]))
    w_loads = []
    for c in range(nc):
        w_loads.append(pltpu.make_async_copy(dw.at[:, pl.ds(c * W, W)], WG.at[c, rep], ld.at[nc + c]))
    h_loads = []
    for k in range(4):
        h_loads.append(pltpu.make_async_copy(hid_in.at[:, k // 2, k % 2], hid.at[:, k % 2, k // 2], ld.at[2 * nc + k]))
    for cp in loads + w_loads + h_loads:
        cp.start()

    peers = [z_dev(k) for k in range(1, 8)] + [x_dev(1), x_dev(-1)] + [yl_dev(k) for k in (1, 2, 3)] + [hc_dev(m) for m in (1, 2, 3)]
    barrier = pltpu.get_barrier_semaphore()
    for p in peers:
        pl.semaphore_signal(barrier, inc=1, device_id=p, device_id_type=MESH)

    idf = ids[...].astype(F32)
    wf = rw[...].astype(F32)
    lane_e = lax.broadcasted_iota(jnp.int32, (128, 128), 1).astype(F32)
    sub_t = lax.broadcasted_iota(jnp.int32, (128, 128), 0).astype(F32)
    named = jnp.zeros((128, 128), F32)
    for k in range(4):
        named = named + jnp.where(idf[:, k : k + 1] == lane_e, 1.0, 0.0)
    before = jnp.where(sub_t > lane_e, 1.0, 0.0)
    count = jnp.dot(before.astype(BF), named.astype(BF), preferred_element_type=F32)
    packed = jnp.zeros((128, 128), F32)
    for k in range(4):
        own = idf[:, k : k + 1]
        rank = jnp.sum(jnp.where(own == lane_e, count, 0.0), axis=1, keepdims=True)
        packed = jnp.where(lane_e == k, own * 32.0 + rank, packed)
        packed = jnp.where(lane_e == 4 + k, wf[:, k : k + 1], packed)
        packed = jnp.where(lane_e == 8 + k, rank, packed)
    CODE[...] = packed
    MT[z, h] = packed.T[0:8, :]

    pl.semaphore_wait(barrier, len(peers))

    def meta_y():
        return remote(MT.at[z, h], MT.at[z, h], ms.at[0], mr.at[0], y_dev)

    def meta_y_in():
        return remote(MT.at[z, ph], MT.at[z, ph], ms.at[0], mr.at[0], y_dev)

    def meta_z(k):
        return remote(MT.at[z], MT.at[z], ms.at[k], mr.at[k], z_dev(k))

    def meta_z_in(k):
        o = (z - k + 8) % 8
        return remote(MT.at[o], MT.at[o], ms.at[k], mr.at[k], z_dev(-k))

    def tok_y(c):
        return remote(G.at[z, h, c], G.at[z, h, c], ys.at[c], yr.at[c], y_dev)

    def tok_y_in(c):
        return remote(G.at[z, ph, c], G.at[z, ph, c], ys.at[c], yr.at[c], y_dev)

    def far(way, d):
        return (z - d + 8) % 8 if way == 0 else (z + d) % 8

    def hi(which):
        return h if which == 0 else ph

    def tok_z(c, which, way, s):
        blk = G.at[far(way, s), hi(which), c]
        return remote(blk, blk, zs.at[c, which, way, s], zr.at[c, which, way, s], z_dev(1 if way == 0 else -1))

    def tok_z_in(c, which, way, s):
        blk = G.at[far(way, s + 1), hi(which), c]
        return remote(blk, blk, zs.at[c, which, way, s], zr.at[c, which, way, s], z_dev(-1 if way == 0 else 1))

    def sends(s):
        return [(0, 0), (0, 1), (1, 0), (1, 1)] if s < 3 else [(0, 0), (1, 1)]

    def swap(c):
        return remote(S.at[c], R.at[c, :, core], cs.at[c], cr.at[c], core_dev)

    def swap_in(c):
        return remote(S.at[c], R.at[c, :, other], cs.at[c], cr.at[c], core_dev)

    def swap_w():
        return remote(WS, WR.at[:, core], cs.at[nc], cr.at[nc], core_dev)

    def swap_w_in():
        return remote(WS, WR.at[:, other], cs.at[nc], cr.at[nc], core_dev)

    def w_y(k):
        return remote(WG.at[:, rep], WG.at[:, rep], wys.at[k - 1], wyr.at[k - 1], yl_dev(k))

    def w_y_in(k):
        o = x * 4 + (yl - k + 4) % 4
        return remote(WG.at[:, o], WG.at[:, o], wys.at[k - 1], wyr.at[k - 1], yl_dev(-k + 4))

    def w_x(way):
        blk = WG.at[:, pl.ds(x * 4, 4)]
        return remote(blk, blk, wxs.at[way], wxr.at[way], x_dev(1 if way == 0 else -1))

    def w_x_in(way):
        o = (x - 1 + 4) % 4 if way == 0 else (x + 1) % 4
        blk = WG.at[:, pl.ds(o * 4, 4)]
        return remote(blk, blk, wxs.at[way], wxr.at[way], x_dev(-1 if way == 0 else 1))

    def w_half(way):
        o = (x - 1 + 4) % 4 if way == 0 else (x + 1) % 4
        blk = WG.at[:, pl.ds(o * 4 + 2 * way, 2)]
        return remote(blk, blk, wxs.at[2 + way], wxr.at[2 + way], x_dev(1 if way == 0 else -1))

    def w_half_in(way):
        o = (x + 2) % 4
        blk = WG.at[:, pl.ds(o * 4 + 2 * way, 2)]
        return remote(blk, blk, wxs.at[2 + way], wxr.at[2 + way], x_dev(-1 if way == 0 else 1))

    x_two, x_up, x_down = (x + 2) % 4, (x + 1) % 4, (x + 3) % 4

    def x_half(c, side):
        return remote(PB.at[c, x_two, side], XH.at[c, side], xhs.at[c, side], xhr.at[c, side], x_dev(-1 if side == 0 else 1))

    def x_full(c, side):
        return remote(PB.at[c, x_down if side == 0 else x_up], XF.at[c, side], xfs.at[c, side], xfr.at[c, side], x_dev(-1 if side == 0 else 1))

    def y_part(c, k):
        return remote(YB.at[c, (yl + k) % 4], YR.at[c, k - 1], yls.at[c, k - 1], ylr.at[c, k - 1], yl_dev(k))

    def score_z(k):
        return remote(SCB.at[(z + k) % 8], L1.at[z], s1s.at[k - 1], s1r.at[k - 1], z_dev(k))

    def score_z_in(k):
        o = (z - k + 8) % 8
        return remote(SCB.at[o], L1.at[o], s1s.at[k - 1], s1r.at[k - 1], z_dev(-k))

    def score_hc(m):
        mine = h * 2 + core
        return remote(TT, L2.at[mine], s2s.at[m - 1], s2r.at[m - 1], hc_dev(m))

    def score_hc_in(m):
        theirs = (ph if m // 2 else h) * 2 + (other if m % 2 else core)
        return remote(TT, L2.at[theirs], s2s.at[m - 1], s2r.at[m - 1], hc_dev(m))

    meta_y().start()
    for c in range(nc):
        loads[c].wait()
        if c == 0:
            tok_y(0).start()
            for way in (0, 1):
                tok_z(0, 0, way, 0).start()
    for c in range(nc):
        w_loads[c].wait()
    for k in (1, 2, 3):
        w_y(k).start()
    meta_y_in().wait_recv()
    for k in range(1, 8):
        meta_z(k).start()

    for k in range(4):
        h_loads[k].wait()

    def turn(q, _):
        blk = hid[q].reshape(128, 1024)
        hidT[q] = blk.T
        return 0

    lax.fori_loop(0, 8, turn, 0)

    def clear(q, _):
        back[q] = jnp.zeros((256, 1024), F32)
        return 0

    lax.fori_loop(0, 4, clear, 0)

    for k in range(1, 8):
        meta_z_in(k).wait_recv()
    expert = (ep * 32).astype(F32)
    expert_other = ((z * 4 + h * 2 + other) * 32).astype(F32)

    def select(n, _):
        zz, hh = n // 2, n % 2
        m = MT[zz, hh]
        row = lax.broadcasted_iota(jnp.int32, (64, 128), 0).astype(F32)
        target = jnp.where(row < 32.0, row + expert, row - 32.0 + expert_other)
        pick = jnp.zeros((64, 128), F32)
        weight = jnp.zeros((64, 128), F32)
        for k in range(4):
            same = m[k : k + 1, :] == target
            pick = jnp.where(same, 1.0, pick)
            weight = jnp.where(same, m[4 + k : 5 + k, :], weight)
        PP[zz, hh] = pick.astype(BF)
        wide = jnp.dot(weight.astype(BF), jnp.ones((128, 128), BF), preferred_element_type=F32).astype(BF)
        WR[zz, core, hh] = wide[0:32]
        WS[zz, hh] = wide[32:64]
        return 0

    lax.fori_loop(0, 16, select, 0)
    swap_w().start()
    swap_w_in().wait_recv()

    def pack(c, zz, hh):
        rows = jnp.dot(PP[zz, hh], G[zz, hh, c], preferred_element_type=F32).astype(BF)
        R[c, zz, core, hh] = rows[0:32]
        S[c, zz, hh] = rows[32:64]

    def forward(c, s):
        for which in (0, 1):
            for way in (0, 1):
                tok_z_in(c, which, way, s - 1).wait_recv()
                if (which, way) in sends(s):
                    tok_z(c, which, way, s).start()

    def pack_far(c, d):
        for which in (0, 1):
            for way in (0, 1):
                pack(c, far(way, d), hi(which))

    def partial(q):
        total = jnp.zeros((256, W), F32)
        for n in range(8):
            total = total + jnp.dot(hidT[n, pl.ds(q * 256, 256)], WB[n], preferred_element_type=F32)
        return total

    def backward(c):
        def rows(q, _):
            r = R[c, pl.ds(q * 2, 2)].reshape(256, W)
            w = WG[c].reshape(1024, W)
            back[q] = back[q] + lax.dot_general(r, w, NT, preferred_element_type=F32)
            return 0

        lax.fori_loop(0, 4, rows, 0)

    def weigh(c):
        def block(n, _):
            wide = WR[n].reshape(128, 128).astype(F32)
            wide = jnp.concatenate([wide] * (W // 128), axis=1)
            WB[n] = (R[c, n].reshape(128, W).astype(F32) * wide).astype(BF)
            return 0

        lax.fori_loop(0, 8, block, 0)

    def turn_of(i, _):
        gather = i < nc
        more = i + 1 < nc
        work = (i >= 1) & (i <= nc)
        a, b, d, f = i, i - 1, i - 2, i - 3

        @pl.when(gather)
        def _():
            tok_y_in(a).wait_recv()
            for way in (0, 1):
                tok_z(a, 1, way, 0).start()

        @pl.when(more)
        def _():
            tok_y(a + 1).start()

        @pl.when(work)
        def _():
            for which, way in sends(3):
                tok_z_in(b, which, way, 3).wait_recv()
            pack(b, (z + 4) % 8, h)
            pack(b, (z + 4) % 8, ph)
            swap(b).start()

        @pl.when(gather)
        def _():
            pack(a, z, h)
            pack(a, z, ph)
            forward(a, 1)
            pack_far(a, 1)

        @pl.when(work)
        def _():
            swap_in(b).wait_recv()
            weigh(b)
            PB[b, x_two] = partial(x_two).astype(BF).reshape(2, 128, W)
            x_half(b, 0).start()
            x_half(b, 1).start()

        @pl.when(gather)
        def _():
            forward(a, 2)

        @pl.when(more)
        def _():
            for way in (0, 1):
                tok_z(a + 1, 0, way, 0).start()

        @pl.when(gather)
        def _():
            pack_far(a, 2)

        @pl.when(i == 0)
        def _():
            for k in (1, 2, 3):
                w_y_in(k).wait_recv()
            w_x(0).start()
            w_x(1).start()

        @pl.when(i == 1)
        def _():
            for way in (0, 1):
                w_x_in(way).wait_recv()
                w_half(way).start()

        @pl.when(i == 2)
        def _():
            for way in (0, 1):
                w_half_in(way).wait_recv()

        @pl.when(work)
        def _():
            TA[...] = partial(x_down)
            TB[...] = partial(x_up)
            OWN[b] = partial(x)
            x_half(b, 0).wait_recv()
            PB[b, x_down, 0] = (TA[0:128] + XH[b, 0].astype(F32)).astype(BF)
            PB[b, x_down, 1] = TA[128:256].astype(BF)
            x_full(b, 0).start()
            x_half(b, 1).wait_recv()
            PB[b, x_up, 0] = TB[0:128].astype(BF)
            PB[b, x_up, 1] = (TB[128:256] + XH[b, 1].astype(F32)).astype(BF)
            x_full(b, 1).start()

        @pl.when(gather)
        def _():
            forward(a, 3)
            pack_far(a, 3)

        @pl.when((i >= 2) & (i <= nc + 1))
        def _():
            x_full(d, 0).wait_recv()
            x_full(d, 1).wait_recv()
            got = XF[d, 0].reshape(256, W).astype(F32) + XF[d, 1].reshape(256, W).astype(F32)
            OWN[d] = OWN[d] + got
            YB[d] = OWN[d].reshape(4, 64, W).astype(BF)
            YO[d] = OWN[d, pl.ds(yl * 64, 64)]
            for k in (1, 2, 3):
                y_part(d, k).start()

        @pl.when((i >= 2) & (i <= nc))
        def _():
            backward(d)

        @pl.when(i == nc)
        def _():
            backward(b)

            def finish(q, _):
                def half(u, _):
                    t = back[q, pl.ds(u * 128, 128)]
                    n = q * 2 + u
                    wide = WR[n].reshape(128, 128).astype(F32)
                    wide = jnp.concatenate([wide] * 8, axis=1)
                    HG[n] = (wide * t).astype(BF).reshape(2, 2, 32, 1024)
                    col = jnp.sum(hid[n].reshape(128, 1024).astype(F32) * t, axis=1, keepdims=True)
                    SCB[n] = jnp.broadcast_to(col, (128, 128)).T[0:8, :]
                    return 0

                lax.fori_loop(0, 2, half, 0)
                return 0

            lax.fori_loop(0, 4, finish, 0)
            for k in range(4):
                pltpu.make_async_copy(HG.at[:, k % 2, k // 2], hg_out.at[:, k // 2, k % 2], out_sem.at[k]).start()
            for k in range(1, 8):
                score_z(k).start()
            L1[z] = SCB[z]

        @pl.when(i == nc + 1)
        def _():
            for k in range(1, 8):
                score_z_in(k).wait_recv()
            sub = lax.broadcasted_iota(jnp.int32, (8, 128), 0)
            tile = jnp.zeros((8, 128), F32)
            for n in range(8):
                tile = jnp.where(sub == n, L1[n], tile)
            TT[...] = tile
            for m in (1, 2, 3):
                score_hc(m).start()
            L2[h * 2 + core] = tile

        @pl.when(i >= 3)
        def _():
            total = YO[f]
            for k in (1, 2, 3):
                y_part(f, k).wait_recv()
                total = total + YR[f, k - 1].astype(F32)
            DG[f] = total.astype(BF)
            pltpu.make_async_copy(DG.at[f], dg_out.at[:, pl.ds(pl.multiple_of(f * W, 128), W)], out_sem.at[4 + f]).start()

        return 0

    lax.fori_loop(0, nc + 3, turn_of, 0)

    for m in (1, 2, 3):
        score_hc_in(m).wait_recv()
    value = L2[...].reshape(32, 128)
    lane32 = lax.broadcasted_iota(jnp.int32, (128, 32), 1)
    order = ((lane32 % 8) * 4 + lane32 // 8).astype(F32)
    lane = lax.broadcasted_iota(jnp.int32, (128, 128), 1).astype(F32)
    mine = ((core * 2 + h) * 32).astype(F32)
    code = CODE[...]
    result = jnp.zeros((128, 128), F32)
    for k in range(4):
        hot = jnp.where(ids[:, k : k + 1].astype(F32) == order, 1.0, 0.0)
        row = jnp.dot(hot, value, preferred_element_type=F32, precision=lax.Precision.HIGHEST)
        got = jnp.sum(jnp.where(lane == mine + code[:, 8 + k : 9 + k], row, 0.0), axis=1, keepdims=True)
        result = jnp.where(lane == k, got, result)
    rg[...] = result[:, 0:4]

    meta_y().wait_send()
    for k in range(1, 8):
        meta_z(k).wait_send()
        score_z(k).wait_send()
    for m in (1, 2, 3):
        score_hc(m).wait_send()
        w_y(m).wait_send()
    for way in (0, 1):
        w_x(way).wait_send()
        w_half(way).wait_send()
    swap_w().wait_send()

    def drain(c, _):
        tok_y(c).wait_send()
        for s in range(4):
            for which, way in sends(s):
                tok_z(c, which, way, s).wait_send()
        swap(c).wait_send()
        for side in (0, 1):
            x_half(c, side).wait_send()
            x_full(c, side).wait_send()
        for k in (1, 2, 3):
            y_part(c, k).wait_send()
        pltpu.make_async_copy(DG.at[c], dg_out.at[:, pl.ds(pl.multiple_of(c * W, 128), W)], out_sem.at[4 + c]).wait()
        return 0

    lax.fori_loop(0, nc, drain, 0)
    for k in range(4):
        pltpu.make_async_copy(HG.at[:, k % 2, k // 2], hg_out.at[:, k // 2, k % 2], out_sem.at[k]).wait()


def on_device(cotangent, expert_ids, route_weight, hidden, down_weight):
    nc = CHUNKS
    width = cotangent.shape[1]
    W = width // nc
    vmem = pltpu.VMEM
    dma = pltpu.SemaphoreType.DMA
    scratch = [
        vmem((8, 2, nc, 128, W), BF),
        vmem((8, 2, 8, 128), F32),
        vmem((8, 2, 64, 128), BF),
        vmem((8, 2, 2, 32, 128), BF),
        vmem((8, 2, 32, 128), BF),
        vmem((nc, 8, 2, 32, W), BF),
        vmem((nc, 8, 2, 2, 32, W), BF),
        vmem((8, 128, W), BF),
        vmem((8, 2, 2, 32, 1024), BF),
        vmem((8, 1024, 128), BF),
        vmem((nc, 16, 64, W), BF),
        vmem((4, 256, 1024), F32),
        vmem((nc, 4, 2, 128, W), BF),
        vmem((256, W), F32),
        vmem((256, W), F32),
        vmem((nc, 256, W), F32),
        vmem((nc, 2, 128, W), BF),
        vmem((nc, 2, 2, 128, W), BF),
        vmem((nc, 4, 64, W), BF),
        vmem((nc, 64, W), F32),
        vmem((nc, 3, 64, W), BF),
        vmem((nc, 64, W), BF),
        vmem((8, 2, 2, 32, 1024), BF),
        vmem((8, 8, 128), F32),
        vmem((8, 8, 128), F32),
        vmem((8, 128), F32),
        vmem((4, 8, 128), F32),
        vmem((128, 128), F32),
        dma((2 * nc + 4,)), dma((nc + 4,)),
        dma((8,)), dma((8,)),
        dma((nc,)), dma((nc,)),
        dma((nc, 2, 2, 4)), dma((nc, 2, 2, 4)),
        dma((nc + 1,)), dma((nc + 1,)),
        dma((3,)), dma((3,)),
        dma((4,)), dma((4,)),
        dma((nc, 2)), dma((nc, 2)),
        dma((nc, 2)), dma((nc, 2)),
        dma((nc, 3)), dma((nc, 3)),
        dma((7,)), dma((7,)),
        dma((3,)), dma((3,)),
    ]
    here = pl.BlockSpec(memory_space=pltpu.VMEM)
    anywhere = pl.BlockSpec(memory_space=pl.ANY)
    router_grad, hidden_grad, down_grad = pl.pallas_call(
        kernel,
        out_shape=(
            jax.ShapeDtypeStruct((128, 4), F32),
            jax.ShapeDtypeStruct((8, 2, 2, 32, 1024), BF),
            jax.ShapeDtypeStruct((64, width), BF),
        ),
        in_specs=[anywhere, here, here, anywhere, anywhere],
        out_specs=(here, anywhere, anywhere),
        scratch_shapes=scratch,
        compiler_params=pltpu.CompilerParams(collective_id=0, has_side_effects=True, vmem_limit_bytes=56 * 2**20),
        cost_estimate=pl.CostEstimate(flops=2 * 2 * 1024 * 1024 * 1536, bytes_accessed=6 * 2**20, transcendentals=0),
    )(cotangent, expert_ids, route_weight, hidden.reshape(8, 2, 2, 32, 1024), down_weight[0])
    return router_grad, hidden_grad.reshape(hidden.shape), down_grad[None]


def solution(mesh):
    in_specs = (
        P(("rep", "ep"), None),
        P(("rep", "ep"), None),
        P(("rep", "ep"), None),
        P("rep", "ep", None, None, None),
        P("ep", "rep", None),
    )
    out_specs = (P(("rep", "ep"), None), P("rep", "ep", None, None, None), P("ep", "rep", None))
    return jax.shard_map(on_device, mesh=mesh, in_specs=in_specs, out_specs=out_specs, check_vma=False)
```

```python
import functools

import jax
import jax.numpy as jnp
from jax import lax
from jax.experimental import pallas as pl
from jax.experimental.pallas import tpu as pltpu
from jax.sharding import PartitionSpec as P

MESH = pl.DeviceIdType.MESH
BF, F32 = jnp.bfloat16, jnp.float32
NT = (((1,), (1,)), ((), ()))
CHUNKS = 4


def remote(src, dst, send, recv, device):
    return pltpu.make_async_remote_copy(
        src_ref=src, dst_ref=dst, send_sem=send, recv_sem=recv, device_id=device, device_id_type=MESH
    )


def kernel(
    ct, ids, rw, hid_in, dw, rg, hg_out, dg_out,
    G, MT, PP, PF, SF, WR, WS, S, R, WB, hid, hidT, WG, back, PB, TA, TB, OWN, XH, XF, YB, YO, YR, DG, HG,
    SCB, L1, HT, MK,
    ld, out_sem, ms, mr, ys, yr, zs, zr, fs, fr, cs, cr, wys, wyr, wxs, wxr, xhs, xhr, xfs, xfr, yls, ylr,
    s1s, s1r,
):
    nc = G.shape[2]
    W = G.shape[4]
    rep, ep = lax.axis_index("rep"), lax.axis_index("ep")
    x, yl = rep // 4, rep % 4
    z, h, core = ep // 4, (ep // 2) % 2, ep % 2
    other = 1 - core
    ph = 1 - h

    def z_dev(k):
        return (rep, ((z + k + 8) % 8) * 4 + h * 2 + core)

    def column_dev(k, o):
        return (rep, ((z + k) % 8) * 4 + (h if o == 0 else ph) * 2 + core)

    def place(m):
        return (ph if m // 2 else h) * 2 + (other if m % 2 else core)

    def group_dev(k, m):
        return (rep, ((z + k) % 8) * 4 + place(m))

    def z_dev_other(k):
        return (rep, ((z + k + 8) % 8) * 4 + h * 2 + other)

    def x_dev(k):
        return (((x + k + 4) % 4) * 4 + yl, ep)

    def yl_dev(k):
        return (x * 4 + (yl + k) % 4, ep)

    def hc_dev(m):
        hh = ph if m // 2 else h
        cc = other if m % 2 else core
        return (rep, z * 4 + hh * 2 + cc)

    core_dev, y_dev = hc_dev(1), hc_dev(2)

    loads = []
    for c in range(nc):
        loads.append(pltpu.make_async_copy(ct.at[:, pl.ds(c * W, W)], G.at[z, h, c], ld.at[c]))
    w_loads = []
    for c in range(nc):
        w_loads.append(pltpu.make_async_copy(dw.at[:, pl.ds(c * W, W)], WG.at[c, rep], ld.at[nc + c]))
    h_loads = []
    for k in range(4):
        h_loads.append(pltpu.make_async_copy(hid_in.at[:, k // 2, k % 2], hid.at[:, k % 2, k // 2], ld.at[2 * nc + k]))
    for cp in loads + w_loads + h_loads:
        cp.start()

    peers = [group_dev(k, m) for k in range(8) for m in range(4) if (k, m) != (0, 0)]
    peers = peers + [x_dev(1), x_dev(-1)] + [yl_dev(k) for k in (1, 2, 3)]
    barrier = pltpu.get_barrier_semaphore()
    for p in peers:
        pl.semaphore_signal(barrier, inc=1, device_id=p, device_id_type=MESH)

    lane_e = lax.broadcasted_iota(jnp.int32, (128, 128), 1).astype(F32)
    sub_t = lax.broadcasted_iota(jnp.int32, (128, 128), 0).astype(F32)
    ids_row, weight_row = ids[...].astype(F32), rw[...].astype(F32)
    rows = jnp.zeros((128, 128), F32)
    for k in range(4):
        rows = jnp.where(sub_t == k, ids_row[k : k + 1], rows)
        rows = jnp.where(sub_t == 4 + k, weight_row[k : k + 1], rows)
    columns = rows.T
    idf, wf = columns[:, 0:4], columns[:, 4:8]
    named = jnp.zeros((128, 128), F32)
    for k in range(4):
        named = named + jnp.where(idf[:, k : k + 1] == lane_e, 1.0, 0.0)
    before = jnp.where(sub_t > lane_e, 1.0, 0.0)
    count = jnp.dot(before.astype(BF), named.astype(BF), preferred_element_type=F32)
    packed = jnp.zeros((128, 128), F32)
    for k in range(4):
        own = idf[:, k : k + 1]
        rank = jnp.sum(jnp.where(own == lane_e, count, 0.0), axis=1, keepdims=True)
        packed = jnp.where(lane_e == k, own * 32.0 + rank, packed)
        packed = jnp.where(lane_e == 4 + k, wf[:, k : k + 1], packed)
        packed = jnp.where(lane_e == 8 + k, rank, packed)
        packed = jnp.where(lane_e == 12 + k, own, packed)
    turned = packed.T
    MT[z, h] = turned[0:8]
    spot = lax.broadcasted_iota(jnp.int32, (256, 128), 0)
    expert_of = jnp.where(spot % 8 == 0, (spot // 32) * 4 + (spot // 8) % 4, -1).astype(F32)
    for k in range(4):
        HT[:, k * 128 : k * 128 + 128] = jnp.where(turned[12 + k : 13 + k] == expert_of, 1.0, 0.0)
        slot = turned[8 + k : 9 + k] + ((core * 2 + h) * 32).astype(F32)
        MK[:, k * 128 : k * 128 + 128] = jnp.where(slot == sub_t, 1.0, 0.0)

    pl.semaphore_wait(barrier, len(peers))

    others = [(k, o) for k in range(8) for o in (0, 1) if (k, o) != (0, 0)]

    def meta(k, o):
        return remote(MT.at[z, h], MT.at[z, h], ms.at[k, o], mr.at[k, o], column_dev(k, o))

    def meta_in(k, o):
        blk = MT.at[(z - k + 8) % 8, h if o == 0 else ph]
        return remote(blk, blk, ms.at[k, o], mr.at[k, o], column_dev(8 - k, o))

    def tok_y(c):
        return remote(G.at[z, h, c], G.at[z, h, c], ys.at[c], yr.at[c], y_dev)

    def tok_y_in(c):
        return remote(G.at[z, ph, c], G.at[z, ph, c], ys.at[c], yr.at[c], y_dev)

    def far(way, d):
        return (z - d + 8) % 8 if way == 0 else (z + d) % 8

    def hi(which):
        return h if which == 0 else ph

    def tok_z(c, which, way, s):
        blk = G.at[far(way, s), hi(which), c]
        return remote(blk, blk, zs.at[c, which, way, s], zr.at[c, which, way, s], z_dev(1 if way == 0 else -1))

    def tok_z_in(c, which, way, s):
        blk = G.at[far(way, s + 1), hi(which), c]
        return remote(blk, blk, zs.at[c, which, way, s], zr.at[c, which, way, s], z_dev(-1 if way == 0 else 1))

    def tok_far(c, way, to):
        k = 1 if way == 0 else -1
        device = z_dev(k) if to == 0 else z_dev_other(k)
        return remote(SF.at[c, way, to], R.at[c, 7, core, hi(way)], fs.at[c, way, to], fr.at[c, way, to], device)

    def tok_far_in(c, way, to):
        k = -1 if way == 0 else 1
        device = z_dev(k) if to == 0 else z_dev_other(k)
        return remote(SF.at[c, way, to], R.at[c, 7, core if to == 0 else other, hi(way)], fs.at[c, way, to], fr.at[c, way, to], device)

    def swap(c):
        return remote(S.at[c], R.at[c, pl.ds(0, 7), core], cs.at[c], cr.at[c], core_dev)

    def swap_in(c):
        return remote(S.at[c], R.at[c, pl.ds(0, 7), other], cs.at[c], cr.at[c], core_dev)

    def plane(n):
        return (z + n + 5) % 8

    def swap_w():
        return remote(WS, WR.at[:, core], cs.at[nc], cr.at[nc], core_dev)

    def swap_w_in():
        return remote(WS, WR.at[:, other], cs.at[nc], cr.at[nc], core_dev)

    def w_y(k):
        blk = WG.at[:, rep]
        return remote(blk, blk, wys.at[k - 1], wyr.at[k - 1], yl_dev(k))

    def w_y_in(k):
        blk = WG.at[:, x * 4 + (yl - k + 4) % 4]
        return remote(blk, blk, wys.at[k - 1], wyr.at[k - 1], yl_dev(4 - k))

    def w_x(k, way):
        blk = WG.at[:, x * 4 + (yl + k) % 4]
        return remote(blk, blk, wxs.at[k, way], wxr.at[k, way], x_dev(1 if way == 0 else -1))

    def w_x_in(k, way):
        o = (x - 1 + 4) % 4 if way == 0 else (x + 1) % 4
        blk = WG.at[:, o * 4 + (yl + k) % 4]
        return remote(blk, blk, wxs.at[k, way], wxr.at[k, way], x_dev(-1 if way == 0 else 1))

    def w_half(k, way):
        o = (x - 1 + 4) % 4 if way == 0 else (x + 1) % 4
        blk = WG.at[:, o * 4 + (yl + k) % 4, pl.ds(32 * way, 32)]
        return remote(blk, blk, wxs.at[k, 2 + way], wxr.at[k, 2 + way], x_dev(1 if way == 0 else -1))

    def w_half_in(k, way):
        o = (x + 2) % 4
        blk = WG.at[:, o * 4 + (yl + k) % 4, pl.ds(32 * way, 32)]
        return remote(blk, blk, wxs.at[k, 2 + way], wxr.at[k, 2 + way], x_dev(-1 if way == 0 else 1))

    x_two, x_up, x_down = (x + 2) % 4, (x + 1) % 4, (x + 3) % 4

    def x_half(c, side):
        return remote(PB.at[c, x_two, side], XH.at[c, side], xhs.at[c, side], xhr.at[c, side], x_dev(-1 if side == 0 else 1))

    def x_full(c, side):
        return remote(PB.at[c, x_down if side == 0 else x_up], XF.at[c, side], xfs.at[c, side], xfr.at[c, side], x_dev(-1 if side == 0 else 1))

    def y_part(c, k):
        return remote(YB.at[c, (yl + k) % 4], YR.at[c, k - 1], yls.at[c, k - 1], ylr.at[c, k - 1], yl_dev(k))

    def score(k, m):
        return remote(SCB.at[(z + k) % 8], L1.at[z, h * 2 + core], s1s.at[k, m], s1r.at[k, m], group_dev(k, m))

    def score_in(k, m):
        o = (z - k + 8) % 8
        return remote(SCB.at[o], L1.at[o, place(m)], s1s.at[k, m], s1r.at[k, m], group_dev(8 - k, m))

    everyone = [(k, m) for k in range(8) for m in range(4) if (k, m) != (0, 0)]

    for k, o in others:
        meta(k, o).start()
    for c in range(nc):
        loads[c].wait()
        if c == 0:
            tok_y(c).start()
        if c < 3:
            for way in (0, 1):
                tok_z(c, 0, way, 0).start()
    for c in range(nc):
        w_loads[c].wait()
    for k in (1, 2, 3):
        w_y(k).start()
    for way in (0, 1):
        w_x(0, way).start()

    def turn(q, _):
        blk = hid[q].reshape(128, 1024)
        hidT[q] = blk.T
        return 0


    def clear(q, _):
        back[q] = jnp.zeros((256, 1024), F32)
        return 0


    row = lax.broadcasted_iota(jnp.int32, (64, 128), 0).astype(F32)

    def match(m, first, second):
        target = jnp.where(row < 32.0, row + first.astype(F32), row - 32.0 + second.astype(F32))
        pick = jnp.zeros((64, 128), F32)
        weight = jnp.zeros((64, 128), F32)
        for k in range(4):
            same = m[k : k + 1, :] == target
            pick = jnp.where(same, 1.0, pick)
            weight = jnp.where(same, m[4 + k : 5 + k, :], weight)
        return pick.astype(BF), weight.astype(BF)

    def select(n, _):
        zz, hh = n // 2, n % 2
        base = (z * 4 + h * 2) * 32
        pick, weight = match(MT[zz, hh], base + core * 32, base + other * 32)
        PP[zz, hh] = pick
        wide = jnp.dot(weight, jnp.ones((128, 128), BF), preferred_element_type=F32).astype(BF)
        WR[zz, core, hh] = wide[0:32]
        WS[zz, hh] = wide[32:64]
        return 0

    def select_far():
        for way in (0, 1):
            base = (((z + 1) % 8 if way == 0 else (z + 7) % 8) * 4 + h * 2) * 32
            PF[way] = match(MT[far(way, 3), hi(way)], base + core * 32, base + other * 32)[0]

    def pack(c, zz, hh, n):
        rows = jnp.dot(PP[zz, hh], G[zz, hh, c], preferred_element_type=F32).astype(BF)
        R[c, n, core, hh] = rows[0:32]
        S[c, n, hh] = rows[32:64]

    def forward(c, s, both=(0, 1)):
        for which in both:
            for way in (0, 1):
                tok_z_in(c, which, way, s - 1).wait_recv()
                if s < 3:
                    tok_z(c, which, way, s).start()
                elif which == way:
                    rows = jnp.dot(PF[way], G[far(way, 3), hi(way), c], preferred_element_type=F32).astype(BF)
                    SF[c, way, 0] = rows[0:32]
                    SF[c, way, 1] = rows[32:64]
                    tok_far(c, way, 0).start()
                    tok_far(c, way, 1).start()

    def pack_far(c, d):
        for which in (0, 1):
            for way in (0, 1):
                pack(c, far(way, d), hi(which), 3 - d if way == 0 else 3 + d)

    def partial(q):
        total = jnp.zeros((256, W), F32)
        for n in range(8):
            total = total + jnp.dot(hidT[plane(n), pl.ds(q * 256, 256)], WB[n], preferred_element_type=F32)
        return total

    def backward(c):
        def rows(q, _):
            r = R[c, pl.ds(q * 2, 2)].reshape(256, W)
            w = WG[c].reshape(1024, W)
            back[q] = back[q] + lax.dot_general(r, w, NT, preferred_element_type=F32)
            return 0

        lax.fori_loop(0, 4, rows, 0)

    def weigh(c):
        def block(n, _):
            wide = WR[plane(n)].reshape(128, 128).astype(F32)
            wide = jnp.concatenate([wide] * (W // 128), axis=1)
            WB[n] = (R[c, n].reshape(128, W).astype(F32) * wide).astype(BF)
            return 0

        lax.fori_loop(0, 8, block, 0)

    def clean(c):
        tok_y(c).wait_send()
        for way in (0, 1):
            for s in range(3):
                tok_z(c, 0, way, s).wait_send()
                tok_z(c, 1, way, s).wait_send()
            for to in (0, 1):
                tok_far(c, way, to).wait_send()
        swap(c).wait_send()
        for side in (0, 1):
            x_half(c, side).wait_send()

    def reduce_y(d):
        x_full(d, 0).wait_recv()
        x_full(d, 1).wait_recv()
        got = XF[d, 0].reshape(256, W).astype(F32) + XF[d, 1].reshape(256, W).astype(F32)
        OWN[d] = OWN[d] + got
        YB[d] = OWN[d].reshape(4, 64, W).astype(BF)
        YO[d] = OWN[d, pl.ds(yl * 64, 64)]
        for k in (1, 2, 3):
            y_part(d, k).start()
        clean(d)

    def turn_of(i, _):
        c, e = i - 4, i - 5
        at = [(i >= s) & (i - s < nc) for s in range(7)]

        @pl.when(i == 0)
        def _():
            forward(0, 1, (0,))

        for s in (3, 2, 1):

            @pl.when((i >= s - 2) & (i - s + 2 < nc))
            def _():
                forward(i - s + 2, s, (0,))

        @pl.when(i + 3 < nc)
        def _():
            for way in (0, 1):
                tok_z(i + 3, 0, way, 0).start()

        for s in (3, 2, 1):

            @pl.when(at[s])
            def _():
                forward(i - s, s, (1,))

        @pl.when(i == nc // 2)
        def _():
            for k in (1, 2, 3):
                w_y_in(k).wait_recv()
                for way in (0, 1):
                    w_x(4 - k, way).start()

        @pl.when(at[0])
        def _():
            tok_y_in(i).wait_recv()
            for way in (0, 1):
                tok_z(i, 1, way, 0).start()

        @pl.when(i + 1 < nc)
        def _():
            tok_y(i + 1).start()

        @pl.when(i == 0)
        def _():
            for k, o in others:
                meta_in(k, o).wait_recv()
            select_far()
            lax.fori_loop(0, 16, select, 0)
            swap_w().start()

        @pl.when(at[4])
        def _():
            swap_in(c).wait_recv()
            for way in (0, 1):
                for to in (0, 1):
                    tok_far_in(c, way, to).wait_recv()
            weigh(c)
            PB[c, x_two] = partial(x_two).astype(BF).reshape(2, 128, W)
            x_half(c, 0).start()
            x_half(c, 1).start()
            TA[c % 2] = partial(x_down)
            TB[c % 2] = partial(x_up)
            OWN[c] = partial(x)

        @pl.when((i >= 7) & (i <= nc + 3))
        def _():
            reduce_y(i - 7)

        for s in (3, 2, 1):

            @pl.when(at[s])
            def _():
                pack_far(i - s, s)

        @pl.when(at[3])
        def _():
            swap(i - 3).start()

        @pl.when(at[0])
        def _():
            pack(i, z, h, 3)
            pack(i, z, ph, 3)

        @pl.when(i == 0)
        def _():
            for k in range(4):
                h_loads[k].wait()
            lax.fori_loop(0, 8, turn, 0)
            lax.fori_loop(0, 4, clear, 0)
            swap_w_in().wait_recv()

        @pl.when(i == 0)
        def _():
            for way in (0, 1):
                w_x_in(0, way).wait_recv()
                w_half(0, way).start()

        @pl.when(i == nc // 2 + 1)
        def _():
            for k in (1, 2, 3):
                for way in (0, 1):
                    w_x_in(k, way).wait_recv()
                    w_half(k, way).start()

        @pl.when(at[5])
        def _():
            x_half(e, 0).wait_recv()
            PB[e, x_down, 0] = (TA[e % 2, 0:128] + XH[e, 0].astype(F32)).astype(BF)
            PB[e, x_down, 1] = TA[e % 2, 128:256].astype(BF)
            x_full(e, 0).start()
            x_half(e, 1).wait_recv()
            PB[e, x_up, 0] = TB[e % 2, 0:128].astype(BF)
            PB[e, x_up, 1] = (TB[e % 2, 128:256] + XH[e, 1].astype(F32)).astype(BF)
            x_full(e, 1).start()

        @pl.when(i == nc + 3)
        def _():
            for k in range(4):
                for way in (0, 1):
                    w_half_in(k, way).wait_recv()
            lax.fori_loop(0, nc // 2, lambda n, _: (backward(n), 0)[1], 0)
            reduce_y(nc - 3)

        @pl.when(i == nc + 4)
        def _():
            lax.fori_loop(nc // 2, nc, lambda n, _: (backward(n), 0)[1], 0)
            reduce_y(nc - 2)

            def finish(q, _):
                def half(u, _):
                    t = back[q, pl.ds(u * 128, 128)]
                    n = plane(q * 2 + u)
                    wide = WR[n].reshape(128, 128).astype(F32)
                    wide = jnp.concatenate([wide] * 8, axis=1)
                    HG[n] = (wide * t).astype(BF).reshape(2, 2, 32, 1024)
                    col = jnp.sum(hid[n].reshape(128, 1024).astype(F32) * t, axis=1, keepdims=True)
                    SCB[n] = jnp.broadcast_to(col, (128, 128)).T[0:8, :]
                    return 0

                lax.fori_loop(0, 2, half, 0)
                return 0

            lax.fori_loop(0, 4, finish, 0)
            for k in range(4):
                pltpu.make_async_copy(HG.at[:, k % 2, k // 2], hg_out.at[:, k // 2, k % 2], out_sem.at[k]).start()
            for k, m in everyone:
                score(k, m).start()
            L1[z, h * 2 + core] = SCB[z]

        return 0

    lax.fori_loop(0, nc + 5, turn_of, 0)
    reduce_y(nc - 1)

    def total_of(f, _):
        total = YO[f]
        for k in (1, 2, 3):
            y_part(f, k).wait_recv()
            total = total + YR[f, k - 1].astype(F32)
        DG[f] = total.astype(BF)
        pltpu.make_async_copy(DG.at[f], dg_out.at[:, pl.ds(pl.multiple_of(f * W, 128), W)], out_sem.at[4 + f]).start()
        return 0

    lax.fori_loop(0, nc, total_of, 0)

    for k, m in everyone:
        score_in(k, m).wait_recv()
    value = L1[...].reshape(256, 128)
    rows = lax.dot_general(value, HT[...], (((0,), (0,)), ((), ())), preferred_element_type=F32, precision=lax.Precision.HIGHEST)
    picked = jnp.sum(rows * MK[...], axis=0, keepdims=True)
    for k in range(4):
        rg[k : k + 1, :] = picked[:, k * 128 : k * 128 + 128]

    for k, o in others:
        meta(k, o).wait_send()
    for k, m in everyone:
        score(k, m).wait_send()
    for k in (1, 2, 3):
        w_y(k).wait_send()
    for k in range(4):
        for way in (0, 1):
            w_x(k, way).wait_send()
            w_half(k, way).wait_send()
    swap_w().wait_send()

    def drain(c, _):
        for side in (0, 1):
            x_full(c, side).wait_send()
        for k in (1, 2, 3):
            y_part(c, k).wait_send()
        pltpu.make_async_copy(DG.at[c], dg_out.at[:, pl.ds(pl.multiple_of(c * W, 128), W)], out_sem.at[4 + c]).wait()
        return 0

    lax.fori_loop(0, nc, drain, 0)
    for k in range(4):
        pltpu.make_async_copy(HG.at[:, k % 2, k // 2], hg_out.at[:, k // 2, k % 2], out_sem.at[k]).wait()


def on_device(cotangent, expert_ids, route_weight, hidden, down_weight):
    nc = CHUNKS
    width = cotangent.shape[1]
    W = width // nc
    vmem = pltpu.VMEM
    dma = pltpu.SemaphoreType.DMA
    scratch = [
        vmem((8, 2, nc, 128, W), BF),
        vmem((8, 2, 8, 128), F32),
        vmem((8, 2, 64, 128), BF),
        vmem((2, 64, 128), BF),
        vmem((nc, 2, 2, 32, W), BF),
        vmem((8, 2, 2, 32, 128), BF),
        vmem((8, 2, 32, 128), BF),
        vmem((nc, 7, 2, 32, W), BF),
        vmem((nc, 8, 2, 2, 32, W), BF),
        vmem((8, 128, W), BF),
        vmem((8, 2, 2, 32, 1024), BF),
        vmem((8, 1024, 128), BF),
        vmem((nc, 16, 64, W), BF),
        vmem((4, 256, 1024), F32),
        vmem((nc, 4, 2, 128, W), BF),
        vmem((2, 256, W), F32),
        vmem((2, 256, W), F32),
        vmem((nc, 256, W), F32),
        vmem((nc, 2, 128, W), BF),
        vmem((nc, 2, 2, 128, W), BF),
        vmem((nc, 4, 64, W), BF),
        vmem((nc, 64, W), F32),
        vmem((nc, 3, 64, W), BF),
        vmem((nc, 64, W), BF),
        vmem((8, 2, 2, 32, 1024), BF),
        vmem((8, 8, 128), F32),
        vmem((8, 4, 8, 128), F32),
        vmem((256, 512), F32),
        vmem((128, 512), F32),
        dma((2 * nc + 4,)), dma((nc + 4,)),
        dma((8, 2)), dma((8, 2)),
        dma((nc,)), dma((nc,)),
        dma((nc, 2, 2, 3)), dma((nc, 2, 2, 3)),
        dma((nc, 2, 2)), dma((nc, 2, 2)),
        dma((nc + 1,)), dma((nc + 1,)),
        dma((3,)), dma((3,)),
        dma((4, 4)), dma((4, 4)),
        dma((nc, 2)), dma((nc, 2)),
        dma((nc, 2)), dma((nc, 2)),
        dma((nc, 3)), dma((nc, 3)),
        dma((8, 4)), dma((8, 4)),
    ]
    here = pl.BlockSpec(memory_space=pltpu.VMEM)
    anywhere = pl.BlockSpec(memory_space=pl.ANY)
    router_grad, hidden_grad, down_grad = pl.pallas_call(
        kernel,
        out_shape=(
            jax.ShapeDtypeStruct((4, 128), F32),
            jax.ShapeDtypeStruct((8, 2, 2, 32, 1024), BF),
            jax.ShapeDtypeStruct((64, width), BF),
        ),
        in_specs=[anywhere, here, here, anywhere, anywhere],
        out_specs=(here, anywhere, anywhere),
        scratch_shapes=scratch,
        compiler_params=pltpu.CompilerParams(collective_id=0, has_side_effects=True, vmem_limit_bytes=56 * 2**20),
        cost_estimate=pl.CostEstimate(flops=2 * 2 * 1024 * 1024 * 1536, bytes_accessed=6 * 2**20, transcendentals=0),
    )(cotangent, expert_ids.T, route_weight.T, hidden.reshape(8, 2, 2, 32, 1024), down_weight[0])
    return router_grad.T, hidden_grad.reshape(hidden.shape), down_grad[None]


def solution(mesh):
    in_specs = (
        P(("rep", "ep"), None),
        P(("rep", "ep"), None),
        P(("rep", "ep"), None),
        P("rep", "ep", None, None, None),
        P("ep", "rep", None),
    )
    out_specs = (P(("rep", "ep"), None), P("rep", "ep", None, None, None), P("ep", "rep", None))
    return jax.shard_map(on_device, mesh=mesh, in_specs=in_specs, out_specs=out_specs, check_vma=False)
```

```python
import functools

import jax
import jax.numpy as jnp
from jax import lax
from jax.experimental import pallas as pl
from jax.experimental.pallas import tpu as pltpu
from jax.sharding import PartitionSpec as P

MESH = pl.DeviceIdType.MESH
BF, F32 = jnp.bfloat16, jnp.float32
NT = (((1,), (1,)), ((), ()))
CHUNKS = 6


def remote(src, dst, send, recv, device):
    return pltpu.make_async_remote_copy(
        src_ref=src, dst_ref=dst, send_sem=send, recv_sem=recv, device_id=device, device_id_type=MESH
    )


def kernel(
    ct, ids, rw, hid_in, dw, rg, hg_out, dg_out,
    G, MT, PP, PF, SF, WR, WS, S, R, WB, hid, hidT, WG, back, PB, TA, TB, OWN, XH, XF, YB, YO, YR, DG, HG,
    SCB, L1, HT, MK,
    ld, out_sem, ms, mr, ys, yr, zs, zr, fs, fr, cs, cr, wys, wyr, wxs, wxr, xhs, xhr, xfs, xfr, yls, ylr,
    s1s, s1r,
):
    nc = G.shape[2]
    W = G.shape[4]
    rep, ep = lax.axis_index("rep"), lax.axis_index("ep")
    x, yl = rep // 4, rep % 4
    z, h, core = ep // 4, (ep // 2) % 2, ep % 2
    other = 1 - core
    ph = 1 - h

    def z_dev(k):
        return (rep, ((z + k + 8) % 8) * 4 + h * 2 + core)

    def column_dev(k, o):
        return (rep, ((z + k) % 8) * 4 + (h if o == 0 else ph) * 2 + core)

    def place(m):
        return (ph if m // 2 else h) * 2 + (other if m % 2 else core)

    def group_dev(k, m):
        return (rep, ((z + k) % 8) * 4 + place(m))

    def z_dev_other(k):
        return (rep, ((z + k + 8) % 8) * 4 + h * 2 + other)

    def x_dev(k):
        return (((x + k + 4) % 4) * 4 + yl, ep)

    def yl_dev(k):
        return (x * 4 + (yl + k) % 4, ep)

    def hc_dev(m):
        hh = ph if m // 2 else h
        cc = other if m % 2 else core
        return (rep, z * 4 + hh * 2 + cc)

    core_dev, y_dev = hc_dev(1), hc_dev(2)

    loads = []
    for c in range(nc):
        loads.append(pltpu.make_async_copy(ct.at[:, pl.ds(c * W, W)], G.at[z, h, c], ld.at[c]))
    w_loads = []
    for c in range(nc):
        w_loads.append(pltpu.make_async_copy(dw.at[:, pl.ds(c * W, W)], WG.at[c, rep], ld.at[nc + c]))
    h_loads = []
    for k in range(4):
        h_loads.append(pltpu.make_async_copy(hid_in.at[:, k // 2, k % 2], hid.at[:, k % 2, k // 2], ld.at[2 * nc + k]))
    for cp in loads + w_loads + h_loads:
        cp.start()

    peers = [group_dev(k, m) for k in range(8) for m in range(4) if (k, m) != (0, 0)]
    peers = peers + [x_dev(1), x_dev(-1)] + [yl_dev(k) for k in (1, 2, 3)]
    barrier = pltpu.get_barrier_semaphore()
    for p in peers:
        pl.semaphore_signal(barrier, inc=1, device_id=p, device_id_type=MESH)

    lane_e = lax.broadcasted_iota(jnp.int32, (128, 128), 1).astype(F32)
    sub_t = lax.broadcasted_iota(jnp.int32, (128, 128), 0).astype(F32)
    ids_row, weight_row = ids[...].astype(F32), rw[...].astype(F32)
    rows = jnp.zeros((128, 128), F32)
    for k in range(4):
        rows = jnp.where(sub_t == k, ids_row[k : k + 1], rows)
        rows = jnp.where(sub_t == 4 + k, weight_row[k : k + 1], rows)
    columns = rows.T
    idf, wf = columns[:, 0:4], columns[:, 4:8]
    named = jnp.zeros((128, 128), F32)
    for k in range(4):
        named = named + jnp.where(idf[:, k : k + 1] == lane_e, 1.0, 0.0)
    before = jnp.where(sub_t > lane_e, 1.0, 0.0)
    count = jnp.dot(before.astype(BF), named.astype(BF), preferred_element_type=F32)
    packed = jnp.zeros((128, 128), F32)
    for k in range(4):
        own = idf[:, k : k + 1]
        rank = jnp.sum(jnp.where(own == lane_e, count, 0.0), axis=1, keepdims=True)
        packed = jnp.where(lane_e == k, own * 32.0 + rank, packed)
        packed = jnp.where(lane_e == 4 + k, wf[:, k : k + 1], packed)
        packed = jnp.where(lane_e == 8 + k, rank, packed)
        packed = jnp.where(lane_e == 12 + k, own, packed)
    turned = packed.T
    MT[z, h] = turned[0:8]
    spot = lax.broadcasted_iota(jnp.int32, (256, 128), 0)
    expert_of = jnp.where(spot % 8 == 0, (spot // 32) * 4 + (spot // 8) % 4, -1).astype(F32)
    for k in range(4):
        HT[:, k * 128 : k * 128 + 128] = jnp.where(turned[12 + k : 13 + k] == expert_of, 1.0, 0.0)
        slot = turned[8 + k : 9 + k] + ((core * 2 + h) * 32).astype(F32)
        MK[:, k * 128 : k * 128 + 128] = jnp.where(slot == sub_t, 1.0, 0.0)

    pl.semaphore_wait(barrier, len(peers))

    others = [(k, o) for k in range(8) for o in (0, 1) if (k, o) != (0, 0)]

    def meta(k, o):
        return remote(MT.at[z, h], MT.at[z, h], ms.at[k, o], mr.at[k, o], column_dev(k, o))

    def meta_in(k, o):
        blk = MT.at[(z - k + 8) % 8, h if o == 0 else ph]
        return remote(blk, blk, ms.at[k, o], mr.at[k, o], column_dev(8 - k, o))

    def tok_y(c):
        return remote(G.at[z, h, c], G.at[z, h, c], ys.at[c], yr.at[c], y_dev)

    def tok_y_in(c):
        return remote(G.at[z, ph, c], G.at[z, ph, c], ys.at[c], yr.at[c], y_dev)

    def far(way, d):
        return (z - d + 8) % 8 if way == 0 else (z + d) % 8

    def hi(which):
        return h if which == 0 else ph

    def tok_z(c, which, way, s):
        blk = G.at[far(way, s), hi(which), c]
        return remote(blk, blk, zs.at[c, which, way, s], zr.at[c, which, way, s], z_dev(1 if way == 0 else -1))

    def tok_z_in(c, which, way, s):
        blk = G.at[far(way, s + 1), hi(which), c]
        return remote(blk, blk, zs.at[c, which, way, s], zr.at[c, which, way, s], z_dev(-1 if way == 0 else 1))

    def tok_far(c, way, to):
        k = 1 if way == 0 else -1
        device = z_dev(k) if to == 0 else z_dev_other(k)
        return remote(SF.at[c, way, to], R.at[c, 7, core, hi(way)], fs.at[c, way, to], fr.at[c, way, to], device)

    def tok_far_in(c, way, to):
        k = -1 if way == 0 else 1
        device = z_dev(k) if to == 0 else z_dev_other(k)
        return remote(SF.at[c, way, to], R.at[c, 7, core if to == 0 else other, hi(way)], fs.at[c, way, to], fr.at[c, way, to], device)

    def swap(c):
        return remote(S.at[c], R.at[c, pl.ds(0, 7), core], cs.at[c], cr.at[c], core_dev)

    def swap_in(c):
        return remote(S.at[c], R.at[c, pl.ds(0, 7), other], cs.at[c], cr.at[c], core_dev)

    def plane(n):
        return (z + n + 5) % 8

    def swap_w():
        return remote(WS, WR.at[:, core], cs.at[nc], cr.at[nc], core_dev)

    def swap_w_in():
        return remote(WS, WR.at[:, other], cs.at[nc], cr.at[nc], core_dev)

    def w_y(k):
        blk = WG.at[:, rep]
        return remote(blk, blk, wys.at[k - 1], wyr.at[k - 1], yl_dev(k))

    def w_y_in(k):
        blk = WG.at[:, x * 4 + (yl - k + 4) % 4]
        return remote(blk, blk, wys.at[k - 1], wyr.at[k - 1], yl_dev(4 - k))

    def w_x(k, way):
        blk = WG.at[:, x * 4 + (yl + k) % 4]
        return remote(blk, blk, wxs.at[k, way], wxr.at[k, way], x_dev(1 if way == 0 else -1))

    def w_x_in(k, way):
        o = (x - 1 + 4) % 4 if way == 0 else (x + 1) % 4
        blk = WG.at[:, o * 4 + (yl + k) % 4]
        return remote(blk, blk, wxs.at[k, way], wxr.at[k, way], x_dev(-1 if way == 0 else 1))

    def w_half(k, way):
        o = (x - 1 + 4) % 4 if way == 0 else (x + 1) % 4
        blk = WG.at[:, o * 4 + (yl + k) % 4, pl.ds(32 * way, 32)]
        return remote(blk, blk, wxs.at[k, 2 + way], wxr.at[k, 2 + way], x_dev(1 if way == 0 else -1))

    def w_half_in(k, way):
        o = (x + 2) % 4
        blk = WG.at[:, o * 4 + (yl + k) % 4, pl.ds(32 * way, 32)]
        return remote(blk, blk, wxs.at[k, 2 + way], wxr.at[k, 2 + way], x_dev(-1 if way == 0 else 1))

    x_two, x_up, x_down = (x + 2) % 4, (x + 1) % 4, (x + 3) % 4

    def x_half(c, side):
        return remote(PB.at[c, x_two, side], XH.at[c, side], xhs.at[c, side], xhr.at[c, side], x_dev(-1 if side == 0 else 1))

    def x_full(c, side):
        return remote(PB.at[c, x_down if side == 0 else x_up], XF.at[c, side], xfs.at[c, side], xfr.at[c, side], x_dev(-1 if side == 0 else 1))

    def y_part(c, k):
        return remote(YB.at[c, (yl + k) % 4], YR.at[c, k - 1], yls.at[c, k - 1], ylr.at[c, k - 1], yl_dev(k))

    def score(k, m):
        return remote(SCB.at[(z + k) % 8], L1.at[z, h * 2 + core], s1s.at[k, m], s1r.at[k, m], group_dev(k, m))

    def score_in(k, m):
        o = (z - k + 8) % 8
        return remote(SCB.at[o], L1.at[o, place(m)], s1s.at[k, m], s1r.at[k, m], group_dev(8 - k, m))

    everyone = [(k, m) for k in range(8) for m in range(4) if (k, m) != (0, 0)]

    for k, o in others:
        meta(k, o).start()
    for c in range(nc):
        loads[c].wait()
        if c == 0:
            tok_y(c).start()
        if c < 3:
            for way in (0, 1):
                tok_z(c, 0, way, 0).start()
    for c in range(nc):
        w_loads[c].wait()
    for way in (0, 1):
        w_x(0, way).start()

    def turn(q, _):
        blk = hid[q].reshape(128, 1024)
        hidT[q] = blk.T
        return 0


    def clear(q, _):
        back[q] = jnp.zeros((256, 1024), F32)
        return 0


    row = lax.broadcasted_iota(jnp.int32, (64, 128), 0).astype(F32)

    def match(m, first, second):
        target = jnp.where(row < 32.0, row + first.astype(F32), row - 32.0 + second.astype(F32))
        pick = jnp.zeros((64, 128), F32)
        weight = jnp.zeros((64, 128), F32)
        for k in range(4):
            same = m[k : k + 1, :] == target
            pick = jnp.where(same, 1.0, pick)
            weight = jnp.where(same, m[4 + k : 5 + k, :], weight)
        return pick.astype(BF), weight.astype(BF)

    def select(n, _):
        zz, hh = n // 2, n % 2
        base = (z * 4 + h * 2) * 32
        pick, weight = match(MT[zz, hh], base + core * 32, base + other * 32)
        PP[zz, hh] = pick
        wide = jnp.dot(weight, jnp.ones((128, 128), BF), preferred_element_type=F32).astype(BF)
        WR[zz, core, hh] = wide[0:32]
        WS[zz, hh] = wide[32:64]
        return 0

    def select_far():
        for way in (0, 1):
            base = (((z + 1) % 8 if way == 0 else (z + 7) % 8) * 4 + h * 2) * 32
            PF[way] = match(MT[far(way, 3), hi(way)], base + core * 32, base + other * 32)[0]

    def pack(c, zz, hh, n):
        rows = jnp.dot(PP[zz, hh], G[zz, hh, c], preferred_element_type=F32).astype(BF)
        R[c, n, core, hh] = rows[0:32]
        S[c, n, hh] = rows[32:64]

    def forward(c, s, both=(0, 1)):
        for which in both:
            for way in (0, 1):
                tok_z_in(c, which, way, s - 1).wait_recv()
                if s < 3:
                    tok_z(c, which, way, s).start()
                elif which == way:
                    rows = jnp.dot(PF[way], G[far(way, 3), hi(way), c], preferred_element_type=F32).astype(BF)
                    SF[c, way, 0] = rows[0:32]
                    SF[c, way, 1] = rows[32:64]
                    tok_far(c, way, 0).start()
                    tok_far(c, way, 1).start()

    def pack_far(c, d):
        for which in (0, 1):
            for way in (0, 1):
                pack(c, far(way, d), hi(which), 3 - d if way == 0 else 3 + d)

    def partial(q):
        total = jnp.zeros((256, W), F32)
        for n in range(8):
            total = total + jnp.dot(hidT[plane(n), pl.ds(q * 256, 256)], WB[n], preferred_element_type=F32)
        return total

    def backward(c):
        def rows(q, _):
            r = R[c, pl.ds(q * 2, 2)].reshape(256, W)
            w = WG[c].reshape(1024, W)
            back[q] = back[q] + lax.dot_general(r, w, NT, preferred_element_type=F32)
            return 0

        lax.fori_loop(0, 4, rows, 0)

    def weigh(c):
        def block(n, _):
            wide = WR[plane(n)].reshape(128, 128).astype(F32)
            wide = jnp.concatenate([wide] * (W // 128), axis=1)
            WB[n] = (R[c, n].reshape(128, W).astype(F32) * wide).astype(BF)
            return 0

        lax.fori_loop(0, 8, block, 0)

    def clean(c):
        tok_y(c).wait_send()
        for way in (0, 1):
            for s in range(3):
                tok_z(c, 0, way, s).wait_send()
                tok_z(c, 1, way, s).wait_send()
            for to in (0, 1):
                tok_far(c, way, to).wait_send()
        swap(c).wait_send()
        for side in (0, 1):
            x_half(c, side).wait_send()

    def send_full(e):
        x_half(e, 0).wait_recv()
        PB[e, x_down, 0] = (TA[e % 3, 0:128] + XH[e, 0].astype(F32)).astype(BF)
        PB[e, x_down, 1] = TA[e % 3, 128:256].astype(BF)
        x_full(e, 0).start()
        x_half(e, 1).wait_recv()
        PB[e, x_up, 0] = TB[e % 3, 0:128].astype(BF)
        PB[e, x_up, 1] = (TB[e % 3, 128:256] + XH[e, 1].astype(F32)).astype(BF)
        x_full(e, 1).start()

    def reduce_y(d):
        x_full(d, 0).wait_recv()
        x_full(d, 1).wait_recv()
        got = XF[d, 0].reshape(256, W).astype(F32) + XF[d, 1].reshape(256, W).astype(F32)
        OWN[d] = OWN[d] + got
        YB[d] = OWN[d].reshape(4, 64, W).astype(BF)
        YO[d] = OWN[d, pl.ds(yl * 64, 64)]
        for k in (1, 2, 3):
            y_part(d, k).start()
        clean(d)

    def turn_of(i, _):
        c = i - 4
        at = [(i >= s) & (i - s < nc) for s in range(7)]

        @pl.when(i == 0)
        def _():
            forward(0, 1, (0,))
            tok_y(1).start()
            w_y(1).start()

        @pl.when(i == 1)
        def _():
            w_y(3).start()

        for s in (3, 2, 1):

            @pl.when((i >= s - 2) & (i - s + 2 < nc))
            def _():
                forward(i - s + 2, s, (0,))

        @pl.when(i + 3 < nc)
        def _():
            for way in (0, 1):
                tok_z(i + 3, 0, way, 0).start()

        for s in (3, 2, 1):

            @pl.when(at[s])
            def _():
                forward(i - s, s, (1,))

        @pl.when(i == nc // 2)
        def _():
            for k in (1, 2, 3):
                w_y_in(k).wait_recv()
                for way in (0, 1):
                    w_x(4 - k, way).start()

        @pl.when(i == nc // 2 + 2)
        def _():
            for k in (1, 2, 3):
                for way in (0, 1):
                    w_x_in(k, way).wait_recv()
                    w_half(k, way).start()

        @pl.when(at[0])
        def _():
            tok_y_in(i).wait_recv()
            for way in (0, 1):
                tok_z(i, 1, way, 0).start()

        @pl.when(i + 2 < nc)
        def _():
            tok_y(i + 2).start()

        @pl.when(i == 0)
        def _():
            w_y(2).start()
            for k, o in others:
                meta_in(k, o).wait_recv()
            select_far()
            lax.fori_loop(0, 16, select, 0)
            swap_w().start()

        @pl.when(at[4])
        def _():
            swap_in(c).wait_recv()
            for way in (0, 1):
                for to in (0, 1):
                    tok_far_in(c, way, to).wait_recv()
            weigh(c)
            PB[c, x_two] = partial(x_two).astype(BF).reshape(2, 128, W)
            x_half(c, 0).start()
            x_half(c, 1).start()

        @pl.when((i >= 6) & (i <= nc + 3))
        def _():
            send_full(i - 6)

        @pl.when(at[4])
        def _():
            TA[c % 3] = partial(x_down)
            TB[c % 3] = partial(x_up)
            OWN[c] = partial(x)

        @pl.when((i >= 8) & (i <= nc + 3))
        def _():
            reduce_y(i - 8)

        for s in (3, 2, 1):

            @pl.when(at[s])
            def _():
                pack_far(i - s, s)

        @pl.when(at[3])
        def _():
            swap(i - 3).start()

        @pl.when(at[0])
        def _():
            pack(i, z, h, 3)
            pack(i, z, ph, 3)

        @pl.when(i == 0)
        def _():
            for k in range(4):
                h_loads[k].wait()
            lax.fori_loop(0, 8, turn, 0)
            lax.fori_loop(0, 4, clear, 0)
            swap_w_in().wait_recv()

        @pl.when(i == 0)
        def _():
            for way in (0, 1):
                w_x_in(0, way).wait_recv()
                w_half(0, way).start()

        @pl.when(i == nc + 3)
        def _():
            send_full(nc - 2)
            for k in range(4):
                for way in (0, 1):
                    w_half_in(k, way).wait_recv()
            lax.fori_loop(0, nc // 2, lambda n, _: (backward(n), 0)[1], 0)
            reduce_y(nc - 4)

        @pl.when(i == nc + 4)
        def _():
            send_full(nc - 1)
            reduce_y(nc - 3)
            lax.fori_loop(nc // 2, nc - 1, lambda n, _: (backward(n), 0)[1], 0)
            reduce_y(nc - 2)
            backward(nc - 1)

            def finish(q, _):
                def half(u, _):
                    t = back[q, pl.ds(u * 128, 128)]
                    n = plane(q * 2 + u)
                    wide = WR[n].reshape(128, 128).astype(F32)
                    wide = jnp.concatenate([wide] * 8, axis=1)
                    HG[n] = (wide * t).astype(BF).reshape(2, 2, 32, 1024)
                    col = jnp.sum(hid[n].reshape(128, 1024).astype(F32) * t, axis=1, keepdims=True)
                    SCB[n] = jnp.broadcast_to(col, (128, 128)).T[0:8, :]
                    return 0

                lax.fori_loop(0, 2, half, 0)
                return 0

            lax.fori_loop(0, 4, finish, 0)
            for k in range(4):
                pltpu.make_async_copy(HG.at[:, k % 2, k // 2], hg_out.at[:, k // 2, k % 2], out_sem.at[k]).start()
            for k, m in everyone:
                score(k, m).start()
            L1[z, h * 2 + core] = SCB[z]

        return 0

    lax.fori_loop(0, nc + 5, turn_of, 0)
    reduce_y(nc - 1)

    def total_of(f, _):
        total = YO[f]
        for k in (1, 2, 3):
            y_part(f, k).wait_recv()
            total = total + YR[f, k - 1].astype(F32)
        DG[f] = total.astype(BF)
        pltpu.make_async_copy(DG.at[f], dg_out.at[:, pl.ds(pl.multiple_of(f * W, 128), W)], out_sem.at[4 + f]).start()
        return 0

    lax.fori_loop(0, nc, total_of, 0)

    for k, m in everyone:
        score_in(k, m).wait_recv()
    value = L1[...].reshape(256, 128)
    rows = lax.dot_general(value, HT[...], (((0,), (0,)), ((), ())), preferred_element_type=F32, precision=lax.Precision.HIGHEST)
    picked = jnp.sum(rows * MK[...], axis=0, keepdims=True)
    for k in range(4):
        rg[k : k + 1, :] = picked[:, k * 128 : k * 128 + 128]

    for k, o in others:
        meta(k, o).wait_send()
    for k, m in everyone:
        score(k, m).wait_send()
    for k in (1, 2, 3):
        w_y(k).wait_send()
    for k in range(4):
        for way in (0, 1):
            w_x(k, way).wait_send()
            w_half(k, way).wait_send()
    swap_w().wait_send()

    def drain(c, _):
        for side in (0, 1):
            x_full(c, side).wait_send()
        for k in (1, 2, 3):
            y_part(c, k).wait_send()
        pltpu.make_async_copy(DG.at[c], dg_out.at[:, pl.ds(pl.multiple_of(c * W, 128), W)], out_sem.at[4 + c]).wait()
        return 0

    lax.fori_loop(0, nc, drain, 0)
    for k in range(4):
        pltpu.make_async_copy(HG.at[:, k % 2, k // 2], hg_out.at[:, k // 2, k % 2], out_sem.at[k]).wait()


def on_device(cotangent, expert_ids, route_weight, hidden, down_weight):
    nc = CHUNKS
    width = cotangent.shape[1]
    W = width // nc
    vmem = pltpu.VMEM
    dma = pltpu.SemaphoreType.DMA
    scratch = [
        vmem((8, 2, nc, 128, W), BF),
        vmem((8, 2, 8, 128), F32),
        vmem((8, 2, 64, 128), BF),
        vmem((2, 64, 128), BF),
        vmem((nc, 2, 2, 32, W), BF),
        vmem((8, 2, 2, 32, 128), BF),
        vmem((8, 2, 32, 128), BF),
        vmem((nc, 7, 2, 32, W), BF),
        vmem((nc, 8, 2, 2, 32, W), BF),
        vmem((8, 128, W), BF),
        vmem((8, 2, 2, 32, 1024), BF),
        vmem((8, 1024, 128), BF),
        vmem((nc, 16, 64, W), BF),
        vmem((4, 256, 1024), F32),
        vmem((nc, 4, 2, 128, W), BF),
        vmem((3, 256, W), F32),
        vmem((3, 256, W), F32),
        vmem((nc, 256, W), F32),
        vmem((nc, 2, 128, W), BF),
        vmem((nc, 2, 2, 128, W), BF),
        vmem((nc, 4, 64, W), BF),
        vmem((nc, 64, W), F32),
        vmem((nc, 3, 64, W), BF),
        vmem((nc, 64, W), BF),
        vmem((8, 2, 2, 32, 1024), BF),
        vmem((8, 8, 128), F32),
        vmem((8, 4, 8, 128), F32),
        vmem((256, 512), F32),
        vmem((128, 512), F32),
        dma((2 * nc + 4,)), dma((nc + 4,)),
        dma((8, 2)), dma((8, 2)),
        dma((nc,)), dma((nc,)),
        dma((nc, 2, 2, 3)), dma((nc, 2, 2, 3)),
        dma((nc, 2, 2)), dma((nc, 2, 2)),
        dma((nc + 1,)), dma((nc + 1,)),
        dma((3,)), dma((3,)),
        dma((4, 4)), dma((4, 4)),
        dma((nc, 2)), dma((nc, 2)),
        dma((nc, 2)), dma((nc, 2)),
        dma((nc, 3)), dma((nc, 3)),
        dma((8, 4)), dma((8, 4)),
    ]
    here = pl.BlockSpec(memory_space=pltpu.VMEM)
    anywhere = pl.BlockSpec(memory_space=pl.ANY)
    router_grad, hidden_grad, down_grad = pl.pallas_call(
        kernel,
        out_shape=(
            jax.ShapeDtypeStruct((4, 128), F32),
            jax.ShapeDtypeStruct((8, 2, 2, 32, 1024), BF),
            jax.ShapeDtypeStruct((64, width), BF),
        ),
        in_specs=[anywhere, here, here, anywhere, anywhere],
        out_specs=(here, anywhere, anywhere),
        scratch_shapes=scratch,
        compiler_params=pltpu.CompilerParams(collective_id=0, has_side_effects=True, vmem_limit_bytes=56 * 2**20),
        cost_estimate=pl.CostEstimate(flops=2 * 2 * 1024 * 1024 * 1536, bytes_accessed=6 * 2**20, transcendentals=0),
    )(cotangent, expert_ids.T, route_weight.T, hidden.reshape(8, 2, 2, 32, 1024), down_weight[0])
    return router_grad.T, hidden_grad.reshape(hidden.shape), down_grad[None]


def solution(mesh):
    in_specs = (
        P(("rep", "ep"), None),
        P(("rep", "ep"), None),
        P(("rep", "ep"), None),
        P("rep", "ep", None, None, None),
        P("ep", "rep", None),
    )
    out_specs = (P(("rep", "ep"), None), P("rep", "ep", None, None, None), P("ep", "rep", None))
    return jax.shard_map(on_device, mesh=mesh, in_specs=in_specs, out_specs=out_specs, check_vma=False)
```

```python
import functools

import jax
import jax.numpy as jnp
from jax import lax
from jax.experimental import pallas as pl
from jax.experimental.pallas import tpu as pltpu
from jax.sharding import PartitionSpec as P

MESH = pl.DeviceIdType.MESH
BF, F32 = jnp.bfloat16, jnp.float32
NT = (((1,), (1,)), ((), ()))
CHUNKS = 6


def remote(src, dst, send, recv, device):
    return pltpu.make_async_remote_copy(
        src_ref=src, dst_ref=dst, send_sem=send, recv_sem=recv, device_id=device, device_id_type=MESH
    )


def kernel(
    ct, ids, rw, hid_in, dw, rg, hg_out, dg_out,
    G, MT, PP, PF, SF, WR, WS, S, R, WB, hid, hidT, WG, back, PB, TA, TB, OWN, XH, XF, YB, YO, YR, DG, HG,
    SCB, L1, HT, MK,
    ld, out_sem, ms, mr, ys, yr, zs, zr, fs, fr, cs, cr, wys, wyr, wxs, wxr, xhs, xhr, xfs, xfr, yls, ylr,
    s1s, s1r,
):
    nc = G.shape[2]
    W = G.shape[4]
    rep, ep = lax.axis_index("rep"), lax.axis_index("ep")
    x, yl = rep // 4, rep % 4
    z, h, core = ep // 4, (ep // 2) % 2, ep % 2
    other = 1 - core
    ph = 1 - h

    def z_dev(k):
        return (rep, ((z + k + 8) % 8) * 4 + h * 2 + core)

    def column_dev(k, o):
        return (rep, ((z + k) % 8) * 4 + (h if o == 0 else ph) * 2 + core)

    def place(m):
        return (ph if m // 2 else h) * 2 + (other if m % 2 else core)

    def group_dev(k, m):
        return (rep, ((z + k) % 8) * 4 + place(m))

    def z_dev_other(k):
        return (rep, ((z + k + 8) % 8) * 4 + h * 2 + other)

    def x_dev(k):
        return (((x + k + 4) % 4) * 4 + yl, ep)

    def yl_dev(k):
        return (x * 4 + (yl + k) % 4, ep)

    def hc_dev(m):
        hh = ph if m // 2 else h
        cc = other if m % 2 else core
        return (rep, z * 4 + hh * 2 + cc)

    core_dev, y_dev = hc_dev(1), hc_dev(2)

    loads = []
    for c in range(nc):
        loads.append(pltpu.make_async_copy(ct.at[:, pl.ds(c * W, W)], G.at[z, h, c], ld.at[c]))
    w_loads = []
    for c in range(nc):
        w_loads.append(pltpu.make_async_copy(dw.at[:, pl.ds(c * W, W)], WG.at[c, rep], ld.at[nc + c]))
    h_loads = []
    for k in range(4):
        h_loads.append(pltpu.make_async_copy(hid_in.at[:, k // 2, k % 2], hid.at[:, k % 2, k // 2], ld.at[2 * nc + k]))
    for cp in loads + w_loads + h_loads:
        cp.start()

    peers = [group_dev(k, m) for k in range(8) for m in range(4) if (k, m) != (0, 0)]
    peers = peers + [x_dev(1), x_dev(-1)] + [yl_dev(k) for k in (1, 2, 3)]
    barrier = pltpu.get_barrier_semaphore()
    for p in peers:
        pl.semaphore_signal(barrier, inc=1, device_id=p, device_id_type=MESH)

    lane_e = lax.broadcasted_iota(jnp.int32, (128, 128), 1).astype(F32)
    sub_t = lax.broadcasted_iota(jnp.int32, (128, 128), 0).astype(F32)
    ids_row, weight_row = ids[...].astype(F32), rw[...].astype(F32)
    rows = jnp.zeros((128, 128), F32)
    for k in range(4):
        rows = jnp.where(sub_t == k, ids_row[k : k + 1], rows)
        rows = jnp.where(sub_t == 4 + k, weight_row[k : k + 1], rows)
    columns = rows.T
    idf, wf = columns[:, 0:4], columns[:, 4:8]
    named = jnp.zeros((128, 128), F32)
    for k in range(4):
        named = named + jnp.where(idf[:, k : k + 1] == lane_e, 1.0, 0.0)
    before = jnp.where(sub_t > lane_e, 1.0, 0.0)
    count = jnp.dot(before.astype(BF), named.astype(BF), preferred_element_type=F32)
    packed = jnp.zeros((128, 128), F32)
    for k in range(4):
        own = idf[:, k : k + 1]
        rank = jnp.sum(jnp.where(own == lane_e, count, 0.0), axis=1, keepdims=True)
        packed = jnp.where(lane_e == k, own * 32.0 + rank, packed)
        packed = jnp.where(lane_e == 4 + k, wf[:, k : k + 1], packed)
        packed = jnp.where(lane_e == 8 + k, rank, packed)
        packed = jnp.where(lane_e == 12 + k, own, packed)
    turned = packed.T
    MT[z, h] = turned[0:8]
    spot = lax.broadcasted_iota(jnp.int32, (256, 128), 0)
    expert_of = jnp.where(spot % 8 == 0, (spot // 32) * 4 + (spot // 8) % 4, -1).astype(F32)
    for k in range(4):
        HT[:, k * 128 : k * 128 + 128] = jnp.where(turned[12 + k : 13 + k] == expert_of, 1.0, 0.0)
        slot = turned[8 + k : 9 + k] + ((core * 2 + h) * 32).astype(F32)
        MK[:, k * 128 : k * 128 + 128] = jnp.where(slot == sub_t, 1.0, 0.0)

    pl.semaphore_wait(barrier, len(peers))

    others = [(k, o) for k in range(8) for o in (0, 1) if (k, o) != (0, 0)]

    def meta(k, o):
        return remote(MT.at[z, h], MT.at[z, h], ms.at[k, o], mr.at[k, o], column_dev(k, o))

    def meta_in(k, o):
        blk = MT.at[(z - k + 8) % 8, h if o == 0 else ph]
        return remote(blk, blk, ms.at[k, o], mr.at[k, o], column_dev(8 - k, o))

    def tok_y(c):
        return remote(G.at[z, h, c], G.at[z, h, c], ys.at[c], yr.at[c], y_dev)

    def tok_y_in(c):
        return remote(G.at[z, ph, c], G.at[z, ph, c], ys.at[c], yr.at[c], y_dev)

    def far(way, d):
        return (z - d + 8) % 8 if way == 0 else (z + d) % 8

    def hi(which):
        return h if which == 0 else ph

    def tok_z(c, which, way, s):
        blk = G.at[far(way, s), hi(which), c]
        return remote(blk, blk, zs.at[c, which, way, s], zr.at[c, which, way, s], z_dev(1 if way == 0 else -1))

    def tok_z_in(c, which, way, s):
        blk = G.at[far(way, s + 1), hi(which), c]
        return remote(blk, blk, zs.at[c, which, way, s], zr.at[c, which, way, s], z_dev(-1 if way == 0 else 1))

    def tok_far(c, way, to):
        k = 1 if way == 0 else -1
        device = z_dev(k) if to == 0 else z_dev_other(k)
        return remote(SF.at[c, way, to], R.at[c, 7, core, hi(way)], fs.at[c, way, to], fr.at[c, way, to], device)

    def tok_far_in(c, way, to):
        k = -1 if way == 0 else 1
        device = z_dev(k) if to == 0 else z_dev_other(k)
        return remote(SF.at[c, way, to], R.at[c, 7, core if to == 0 else other, hi(way)], fs.at[c, way, to], fr.at[c, way, to], device)

    def swap(c):
        return remote(S.at[c], R.at[c, pl.ds(0, 7), core], cs.at[c], cr.at[c], core_dev)

    def swap_in(c):
        return remote(S.at[c], R.at[c, pl.ds(0, 7), other], cs.at[c], cr.at[c], core_dev)

    def plane(n):
        return (z + n + 5) % 8

    def swap_w():
        return remote(WS, WR.at[:, core], cs.at[nc], cr.at[nc], core_dev)

    def swap_w_in():
        return remote(WS, WR.at[:, other], cs.at[nc], cr.at[nc], core_dev)

    def w_y(k):
        blk = WG.at[:, rep]
        return remote(blk, blk, wys.at[k - 1], wyr.at[k - 1], yl_dev(k))

    def w_y_in(k):
        blk = WG.at[:, x * 4 + (yl - k + 4) % 4]
        return remote(blk, blk, wys.at[k - 1], wyr.at[k - 1], yl_dev(4 - k))

    def w_x(k, way):
        blk = WG.at[:, x * 4 + (yl + k) % 4]
        return remote(blk, blk, wxs.at[k, way], wxr.at[k, way], x_dev(1 if way == 0 else -1))

    def w_x_in(k, way):
        o = (x - 1 + 4) % 4 if way == 0 else (x + 1) % 4
        blk = WG.at[:, o * 4 + (yl + k) % 4]
        return remote(blk, blk, wxs.at[k, way], wxr.at[k, way], x_dev(-1 if way == 0 else 1))

    def w_half(k, way):
        o = (x - 1 + 4) % 4 if way == 0 else (x + 1) % 4
        blk = WG.at[:, o * 4 + (yl + k) % 4, pl.ds(32 * way, 32)]
        return remote(blk, blk, wxs.at[k, 2 + way], wxr.at[k, 2 + way], x_dev(1 if way == 0 else -1))

    def w_half_in(k, way):
        o = (x + 2) % 4
        blk = WG.at[:, o * 4 + (yl + k) % 4, pl.ds(32 * way, 32)]
        return remote(blk, blk, wxs.at[k, 2 + way], wxr.at[k, 2 + way], x_dev(-1 if way == 0 else 1))

    x_two, x_up, x_down = (x + 2) % 4, (x + 1) % 4, (x + 3) % 4

    def x_half(c, side):
        return remote(PB.at[c, x_two, side], XH.at[c, side], xhs.at[c, side], xhr.at[c, side], x_dev(-1 if side == 0 else 1))

    def x_full(c, side):
        return remote(PB.at[c, x_down if side == 0 else x_up], XF.at[c, side], xfs.at[c, side], xfr.at[c, side], x_dev(-1 if side == 0 else 1))

    def y_part(c, k):
        return remote(YB.at[c, (yl + k) % 4], YR.at[c, k - 1], yls.at[c, k - 1], ylr.at[c, k - 1], yl_dev(k))

    def score(k, m):
        return remote(SCB.at[(z + k) % 8], L1.at[z, h * 2 + core], s1s.at[k, m], s1r.at[k, m], group_dev(k, m))

    def score_in(k, m):
        o = (z - k + 8) % 8
        return remote(SCB.at[o], L1.at[o, place(m)], s1s.at[k, m], s1r.at[k, m], group_dev(8 - k, m))

    everyone = [(k, m) for k in range(8) for m in range(4) if (k, m) != (0, 0)]

    for k, o in others:
        meta(k, o).start()
    for c in range(nc):
        loads[c].wait()
        if c == 0:
            tok_y(c).start()
        if c < 3:
            for way in (0, 1):
                tok_z(c, 0, way, 0).start()
    for c in range(nc):
        w_loads[c].wait()
    for way in (0, 1):
        w_x(0, way).start()

    def turn(q, _):
        blk = hid[q].reshape(128, 1024)
        hidT[q] = blk.T
        return 0


    def clear(q, _):
        back[q] = jnp.zeros((256, 1024), F32)
        return 0


    row = lax.broadcasted_iota(jnp.int32, (64, 128), 0).astype(F32)

    def match(m, first, second):
        target = jnp.where(row < 32.0, row + first.astype(F32), row - 32.0 + second.astype(F32))
        pick = jnp.zeros((64, 128), F32)
        weight = jnp.zeros((64, 128), F32)
        for k in range(4):
            same = m[k : k + 1, :] == target
            pick = jnp.where(same, 1.0, pick)
            weight = jnp.where(same, m[4 + k : 5 + k, :], weight)
        return pick.astype(BF), weight.astype(BF)

    def select(n, _):
        zz, hh = n // 2, n % 2
        base = (z * 4 + h * 2) * 32
        pick, weight = match(MT[zz, hh], base + core * 32, base + other * 32)
        PP[zz, hh] = pick
        wide = jnp.dot(weight, jnp.ones((128, 128), BF), preferred_element_type=F32).astype(BF)
        WR[zz, core, hh] = wide[0:32]
        WS[zz, hh] = wide[32:64]
        return 0

    def select_far():
        for way in (0, 1):
            base = (((z + 1) % 8 if way == 0 else (z + 7) % 8) * 4 + h * 2) * 32
            PF[way] = match(MT[far(way, 3), hi(way)], base + core * 32, base + other * 32)[0]

    def pack(c, zz, hh, n):
        rows = jnp.dot(PP[zz, hh], G[zz, hh, c], preferred_element_type=F32).astype(BF)
        R[c, n, core, hh] = rows[0:32]
        S[c, n, hh] = rows[32:64]

    def forward(c, s, both=(0, 1)):
        for which in both:
            for way in (0, 1):
                tok_z_in(c, which, way, s - 1).wait_recv()
                if s < 3:
                    tok_z(c, which, way, s).start()
                elif which == way:
                    rows = jnp.dot(PF[way], G[far(way, 3), hi(way), c], preferred_element_type=F32).astype(BF)
                    SF[c, way, 0] = rows[0:32]
                    SF[c, way, 1] = rows[32:64]
                    tok_far(c, way, 0).start()
                    tok_far(c, way, 1).start()

    def pack_far(c, d):
        for which in (0, 1):
            for way in (0, 1):
                pack(c, far(way, d), hi(which), 3 - d if way == 0 else 3 + d)

    def partial(q):
        total = jnp.zeros((256, W), F32)
        for n in range(8):
            total = total + jnp.dot(hidT[plane(n), pl.ds(q * 256, 256)], WB[n], preferred_element_type=F32)
        return total

    def backward(c):
        def rows(q, _):
            r = R[c, pl.ds(q * 2, 2)].reshape(256, W)
            w = WG[c].reshape(1024, W)
            back[q] = back[q] + lax.dot_general(r, w, NT, preferred_element_type=F32)
            return 0

        lax.fori_loop(0, 4, rows, 0)

    def weigh(c):
        def block(n, _):
            wide = WR[plane(n)].reshape(128, 128).astype(F32)
            wide = jnp.concatenate([wide] * (W // 128), axis=1)
            WB[n] = (R[c, n].reshape(128, W).astype(F32) * wide).astype(BF)
            return 0

        lax.fori_loop(0, 8, block, 0)

    def clean(c):
        tok_y(c).wait_send()
        for way in (0, 1):
            for s in range(3):
                tok_z(c, 0, way, s).wait_send()
                tok_z(c, 1, way, s).wait_send()
            for to in (0, 1):
                tok_far(c, way, to).wait_send()
        swap(c).wait_send()
        for side in (0, 1):
            x_half(c, side).wait_send()

    def send_full(e):
        x_half(e, 0).wait_recv()
        PB[e, x_down, 0] = (TA[e % 3, 0:128] + XH[e, 0].astype(F32)).astype(BF)
        PB[e, x_down, 1] = TA[e % 3, 128:256].astype(BF)
        x_full(e, 0).start()
        x_half(e, 1).wait_recv()
        PB[e, x_up, 0] = TB[e % 3, 0:128].astype(BF)
        PB[e, x_up, 1] = (TB[e % 3, 128:256] + XH[e, 1].astype(F32)).astype(BF)
        x_full(e, 1).start()

    def reduce_y(d):
        x_full(d, 0).wait_recv()
        x_full(d, 1).wait_recv()
        got = XF[d, 0].reshape(256, W).astype(F32) + XF[d, 1].reshape(256, W).astype(F32)
        OWN[d] = OWN[d] + got
        YB[d] = OWN[d].reshape(4, 64, W).astype(BF)
        YO[d] = OWN[d, pl.ds(yl * 64, 64)]
        for k in (1, 2, 3):
            y_part(d, k).start()
        clean(d)

    def turn_of(i, _):
        c = i - 4
        at = [(i >= s) & (i - s < nc) for s in range(7)]

        @pl.when(i == 0)
        def _():
            forward(0, 1, (0,))
            tok_y(1).start()
            w_y(1).start()

        @pl.when(i == 1)
        def _():
            w_y(3).start()

        for s in (3, 2, 1):

            @pl.when((i >= s - 2) & (i - s + 2 < nc))
            def _():
                forward(i - s + 2, s, (0,))

        @pl.when(i + 3 < nc)
        def _():
            for way in (0, 1):
                tok_z(i + 3, 0, way, 0).start()

        for s in (3, 2, 1):

            @pl.when(at[s])
            def _():
                forward(i - s, s, (1,))

        @pl.when(i == nc // 2)
        def _():
            for k in (1, 2, 3):
                w_y_in(k).wait_recv()
                for way in (0, 1):
                    w_x(4 - k, way).start()

        @pl.when(i == nc // 2 + 2)
        def _():
            for k in (1, 2, 3):
                for way in (0, 1):
                    w_x_in(k, way).wait_recv()
                    w_half(k, way).start()

        @pl.when(at[0])
        def _():
            tok_y_in(i).wait_recv()
            for way in (0, 1):
                tok_z(i, 1, way, 0).start()

        @pl.when(i + 2 < nc)
        def _():
            tok_y(i + 2).start()

        @pl.when(i == 0)
        def _():
            w_y(2).start()
            for k, o in others:
                meta_in(k, o).wait_recv()
            select_far()
            lax.fori_loop(0, 16, select, 0)
            swap_w().start()

        @pl.when(at[4])
        def _():
            swap_in(c).wait_recv()
            for way in (0, 1):
                for to in (0, 1):
                    tok_far_in(c, way, to).wait_recv()
            weigh(c)
            PB[c, x_two] = partial(x_two).astype(BF).reshape(2, 128, W)
            x_half(c, 0).start()
            x_half(c, 1).start()

        @pl.when((i >= 6) & (i <= nc + 3))
        def _():
            send_full(i - 6)

        @pl.when(at[4])
        def _():
            TA[c % 3] = partial(x_down)
            TB[c % 3] = partial(x_up)
            OWN[c] = partial(x)

        @pl.when((i >= 8) & (i <= nc + 3))
        def _():
            reduce_y(i - 8)

        for s in (3, 2, 1):

            @pl.when(at[s])
            def _():
                pack_far(i - s, s)

        @pl.when(at[3])
        def _():
            swap(i - 3).start()

        @pl.when(at[0])
        def _():
            pack(i, z, h, 3)
            pack(i, z, ph, 3)

        @pl.when(i == 0)
        def _():
            for k in range(4):
                h_loads[k].wait()
            lax.fori_loop(0, 8, turn, 0)
            lax.fori_loop(0, 4, clear, 0)
            swap_w_in().wait_recv()

        @pl.when(i == 0)
        def _():
            for way in (0, 1):
                w_x_in(0, way).wait_recv()
                w_half(0, way).start()

        @pl.when(i == nc + 2)
        def _():
            for k in range(4):
                for way in (0, 1):
                    w_half_in(k, way).wait_recv()
            backward(0)

        @pl.when(i == nc + 3)
        def _():
            send_full(nc - 2)
            lax.fori_loop(1, nc // 2, lambda n, _: (backward(n), 0)[1], 0)
            reduce_y(nc - 4)

        @pl.when(i == nc + 4)
        def _():
            send_full(nc - 1)
            reduce_y(nc - 3)
            lax.fori_loop(nc // 2, nc - 1, lambda n, _: (backward(n), 0)[1], 0)
            reduce_y(nc - 2)
            backward(nc - 1)

            def finish(q, _):
                def half(u, _):
                    t = back[q, pl.ds(u * 128, 128)]
                    n = plane(q * 2 + u)
                    wide = WR[n].reshape(128, 128).astype(F32)
                    wide = jnp.concatenate([wide] * 8, axis=1)
                    HG[n] = (wide * t).astype(BF).reshape(2, 2, 32, 1024)
                    col = jnp.sum(hid[n].reshape(128, 1024).astype(F32) * t, axis=1, keepdims=True)
                    SCB[n] = jnp.broadcast_to(col, (128, 128)).T[0:8, :]
                    return 0

                lax.fori_loop(0, 2, half, 0)
                return 0

            lax.fori_loop(0, 4, finish, 0)
            for k in range(4):
                pltpu.make_async_copy(HG.at[:, k % 2, k // 2], hg_out.at[:, k // 2, k % 2], out_sem.at[k]).start()
            for k, m in everyone:
                score(k, m).start()
            L1[z, h * 2 + core] = SCB[z]

        return 0

    lax.fori_loop(0, nc + 5, turn_of, 0)
    reduce_y(nc - 1)

    def total_of(f, _):
        total = YO[f]
        for k in (1, 2, 3):
            y_part(f, k).wait_recv()
            total = total + YR[f, k - 1].astype(F32)
        DG[f] = total.astype(BF)
        pltpu.make_async_copy(DG.at[f], dg_out.at[:, pl.ds(pl.multiple_of(f * W, 128), W)], out_sem.at[4 + f]).start()
        return 0

    lax.fori_loop(0, nc, total_of, 0)

    for k, m in everyone:
        score_in(k, m).wait_recv()
    value = L1[...].reshape(256, 128)
    rows = lax.dot_general(value, HT[...], (((0,), (0,)), ((), ())), preferred_element_type=F32, precision=lax.Precision.HIGHEST)
    picked = jnp.sum(rows * MK[...], axis=0, keepdims=True)
    for k in range(4):
        rg[k : k + 1, :] = picked[:, k * 128 : k * 128 + 128]

    for k, o in others:
        meta(k, o).wait_send()
    for k, m in everyone:
        score(k, m).wait_send()
    for k in (1, 2, 3):
        w_y(k).wait_send()
    for k in range(4):
        for way in (0, 1):
            w_x(k, way).wait_send()
            w_half(k, way).wait_send()
    swap_w().wait_send()

    def drain(c, _):
        for side in (0, 1):
            x_full(c, side).wait_send()
        for k in (1, 2, 3):
            y_part(c, k).wait_send()
        pltpu.make_async_copy(DG.at[c], dg_out.at[:, pl.ds(pl.multiple_of(c * W, 128), W)], out_sem.at[4 + c]).wait()
        return 0

    lax.fori_loop(0, nc, drain, 0)
    for k in range(4):
        pltpu.make_async_copy(HG.at[:, k % 2, k // 2], hg_out.at[:, k // 2, k % 2], out_sem.at[k]).wait()


def on_device(cotangent, expert_ids, route_weight, hidden, down_weight):
    nc = CHUNKS
    width = cotangent.shape[1]
    W = width // nc
    vmem = pltpu.VMEM
    dma = pltpu.SemaphoreType.DMA
    scratch = [
        vmem((8, 2, nc, 128, W), BF),
        vmem((8, 2, 8, 128), F32),
        vmem((8, 2, 64, 128), BF),
        vmem((2, 64, 128), BF),
        vmem((nc, 2, 2, 32, W), BF),
        vmem((8, 2, 2, 32, 128), BF),
        vmem((8, 2, 32, 128), BF),
        vmem((nc, 7, 2, 32, W), BF),
        vmem((nc, 8, 2, 2, 32, W), BF),
        vmem((8, 128, W), BF),
        vmem((8, 2, 2, 32, 1024), BF),
        vmem((8, 1024, 128), BF),
        vmem((nc, 16, 64, W), BF),
        vmem((4, 256, 1024), F32),
        vmem((nc, 4, 2, 128, W), BF),
        vmem((3, 256, W), F32),
        vmem((3, 256, W), F32),
        vmem((nc, 256, W), F32),
        vmem((nc, 2, 128, W), BF),
        vmem((nc, 2, 2, 128, W), BF),
        vmem((nc, 4, 64, W), BF),
        vmem((nc, 64, W), F32),
        vmem((nc, 3, 64, W), BF),
        vmem((nc, 64, W), BF),
        vmem((8, 2, 2, 32, 1024), BF),
        vmem((8, 8, 128), F32),
        vmem((8, 4, 8, 128), F32),
        vmem((256, 512), F32),
        vmem((128, 512), F32),
        dma((2 * nc + 4,)), dma((nc + 4,)),
        dma((8, 2)), dma((8, 2)),
        dma((nc,)), dma((nc,)),
        dma((nc, 2, 2, 3)), dma((nc, 2, 2, 3)),
        dma((nc, 2, 2)), dma((nc, 2, 2)),
        dma((nc + 1,)), dma((nc + 1,)),
        dma((3,)), dma((3,)),
        dma((4, 4)), dma((4, 4)),
        dma((nc, 2)), dma((nc, 2)),
        dma((nc, 2)), dma((nc, 2)),
        dma((nc, 3)), dma((nc, 3)),
        dma((8, 4)), dma((8, 4)),
    ]
    here = pl.BlockSpec(memory_space=pltpu.VMEM)
    anywhere = pl.BlockSpec(memory_space=pl.ANY)
    router_grad, hidden_grad, down_grad = pl.pallas_call(
        kernel,
        out_shape=(
            jax.ShapeDtypeStruct((4, 128), F32),
            jax.ShapeDtypeStruct((8, 2, 2, 32, 1024), BF),
            jax.ShapeDtypeStruct((64, width), BF),
        ),
        in_specs=[anywhere, here, here, anywhere, anywhere],
        out_specs=(here, anywhere, anywhere),
        scratch_shapes=scratch,
        compiler_params=pltpu.CompilerParams(collective_id=0, has_side_effects=True, vmem_limit_bytes=56 * 2**20),
        cost_estimate=pl.CostEstimate(flops=2 * 2 * 1024 * 1024 * 1536, bytes_accessed=6 * 2**20, transcendentals=0),
    )(cotangent, expert_ids.T, route_weight.T, hidden.reshape(8, 2, 2, 32, 1024), down_weight[0])
    return router_grad.T, hidden_grad.reshape(hidden.shape), down_grad[None]


def solution(mesh):
    in_specs = (
        P(("rep", "ep"), None),
        P(("rep", "ep"), None),
        P(("rep", "ep"), None),
        P("rep", "ep", None, None, None),
        P("ep", "rep", None),
    )
    out_specs = (P(("rep", "ep"), None), P("rep", "ep", None, None, None), P("ep", "rep", None))
    return jax.shard_map(on_device, mesh=mesh, in_specs=in_specs, out_specs=out_specs, check_vma=False)
```
